32 devices in a mesh: groups: 2 (over x), dev: 16 (over z, y, core).
Axes of the slice: x: 2, y: 2, z: 4, core: 2. Of those that a mesh axis runs over, the one named last changes fastest.
Arguments:
- x_in: bfloat16 [2, 64, 3072], P(None, ('groups', 'dev')), parts along dimension 1, may hold values from -6 to 6
- queries: bfloat16 [2, 64, 3072], P(None, ('groups', 'dev')), parts along dimension 1, may hold values from -75 to 75
- cache_keys: bfloat16 [2, 64, 128, 512], P(None, ('groups', 'dev')), parts along dimension 1, may hold values from -6 to 6
- cache_values: bfloat16 [2, 64, 128, 512], P(None, ('groups', 'dev')), parts along dimension 1, may hold values from -6 to 6
- new_keys: bfloat16 [2, 64, 512], P(None, ('groups', 'dev')), parts along dimension 1, may hold values from -6 to 6
- new_values: bfloat16 [2, 64, 512], P(None, ('groups', 'dev')), parts along dimension 1, may hold values from -6 to 6
- lengths: int32 [2, 64], P(None, ('groups', 'dev')), parts along dimension 1, may hold values from 1 to 128
- w_out: bfloat16 [3072, 3072], P('dev'), may hold values from -0.109375 to 0.109375
- norm_gain: bfloat16 [3072], replicated, may hold values from 0.25 to 1.75
- w_router: bfloat16 [3072, 4], replicated, may hold values from -0.3125 to 0.3125
- experts_idx: int32 [2, 64, 2], P(None, ('groups', 'dev')), parts along dimension 1, may hold values from 0 to 3, all different within a row; in each aligned block of 2 rows (0 to 1, 2 to 3, ..., all dimensions but the last counted through in order) at most 2 rows name the same one
- w_gate: bfloat16 [3072, 32768], P(None, 'dev'), may hold values from -0.109375 to 0.109375
- w_up: bfloat16 [3072, 32768], P(None, 'dev'), may hold values from -0.109375 to 0.109375
- w_down: bfloat16 [32768, 3072], P('dev'), may hold values from -0.0625 to 0.0625
Outputs:
- mixed: bfloat16 [2, 64, 3072], P(None, ('groups', 'dev')), parts along dimension 1
The draws below stay inside these ranges and needn't reach their ends.
There are 2 independent parts, one for each index of `groups`. The reference program is written for one: setup_inputs(seed, part) draws one part's arguments, and reference() takes and returns one part's arrays. A program takes and returns all parts, laid end to end along the dimension named above; an argument that names none is the same for every part. Nothing has to cross between parts.
All inputs are finite; a program needn't handle non-finite values.
Results may differ from the reference program's by a relative error of at most 0.006.
Values may be sent and summed in bfloat16 or wider, within the bound.
No kernel may reach another device: no remote copies, remote signals or barrier semaphores. Data moves between devices by JAX's collectives and lax.ppermute only.
A program may use at most 128 MiB of HBM per device.

```python
import math
import jax
import jax.numpy as jnp
import numpy as np
from jax import lax

D = 3072
QH = 24
KVH = 4
HD = 128
E = 4
FF = 8192
TOPK = 2
MB = 2
S_DEV = 2
LEN = 128
ROWS = 32


def draw_queries(key, part):
    key = jax.random.fold_in(key, 7)
    base_values = jnp.clip(jax.random.normal(key, (MB, ROWS, QH * HD), jnp.float32), -6.0, 6.0)
    return base_values.astype(jnp.bfloat16)


def draw_cache_keys(key, part):
    key = jax.random.fold_in(key, 11)
    base_values = jnp.clip(jax.random.normal(key, (MB, ROWS, LEN, KVH * HD), jnp.float32), -6.0, 6.0)
    return base_values.astype(jnp.bfloat16)


def set_ends(entries, rng, low, largest):
    longest = entries.shape.index(max(entries.shape))
    spots = []
    for shift in (0, 1):
        where = [jax.random.randint(jax.random.fold_in(rng, axis), (), 0, length) for axis, length in enumerate(entries.shape)]
        where[longest] = (where[longest] + shift) % entries.shape[longest]
        spots.append(tuple(where))
    return entries.at[spots[0]].set(low).at[spots[1]].set(largest)


def block_levels(key, extent, shards, smallest, largest):
    def one(position, blocks):
        draws = jax.random.uniform(jax.random.fold_in(jax.random.fold_in(key, 6), position), (blocks,), jnp.float32, smallest / len(shards), largest / len(shards))
        return jnp.repeat(jnp.exp(draws), extent[position] // blocks).reshape((-1,) + (1,) * (len(extent) - position - 1))

    loudness = one(*shards[0])
    for cut in shards[1:]:
        loudness = loudness * one(*cut)
    return loudness


def deal_out(key, own, number, rows, amount, top, most, skew):
    ranking = jax.random.permutation(key, amount)
    packed, ordinary = portions_of(amount, rows * top, most, skew, True), portions_of(amount, rows * top, most, skew, False)
    places = jnp.arange(amount)

    def named(tallies, rotation):
        used = int((tallies > 0).sum())
        fixed = max(1, used // 4)
        moved = fixed + (places - fixed + rotation * (used - fixed)) % max(1, amount - fixed)
        return jnp.zeros((amount,), jnp.int32).at[ranking[jnp.where(places < fixed, places, moved)]].set(jnp.asarray(tallies, jnp.int32))

    tallies = jnp.where(number % 4 == 0, named(packed, number // 4), named(ordinary, number - number // 4 - 1))
    mixed = jax.random.permutation(jax.random.fold_in(own, 3), amount)
    source_of, sink = mixed[0:amount // 2 * 2:2], mixed[1:amount // 2 * 2:2]
    room = jnp.minimum(tallies[source_of] - 1, most - tallies[sink]) // 2
    room = jnp.where((source_of == ranking[0]) | (sink == ranking[0]) | (tallies[sink] == 0), 0, jnp.maximum(room, 0))
    moved = jax.random.randint(jax.random.fold_in(own, 4), (amount // 2,), 0, 1 << 20) % (room + 1)
    tallies = tallies.at[source_of].add(-moved).at[sink].add(moved)
    labels = jnp.searchsorted(jnp.cumsum(tallies), jnp.arange(rows * top), side="right").astype(jnp.int32)
    listing = labels.reshape(top, rows).T
    listing = listing[jax.random.permutation(jax.random.fold_in(own, 1), rows)]
    rotation = jax.random.randint(jax.random.fold_in(own, 2), (rows, 1), 0, top)
    return jnp.take_along_axis(listing, (jnp.arange(top)[None, :] + rotation) % top, axis=1)


def portions_of(amount, total, bound, slope, full):
    loads = [(1 << 20) // math.isqrt(rank ** slope) + 1 for rank in range(1, amount + 1)]
    largest = bound if full else min(bound, max(-(-total // amount), total * loads[0] // sum(loads)))
    least = 1 if total - largest >= amount - 1 else 0
    holding, rest = [largest] + [least] * (amount - 1), total - largest - least * (amount - 1)
    while rest > 0:
        candidates = [i for i in range(1, amount) if holding[i] < largest] or [i for i in range(1, amount) if holding[i] < bound]
        mass, left = sum([loads[i] for i in candidates]), rest
        for i in candidates:
            addition = min(bound - holding[i], max(1, left * loads[i] // mass), rest)
            holding[i] = holding[i] + addition
            rest = rest - addition
    return np.array(holding)


def scatter_about(own_key, shape, deviation, bound, cuts=(), held_as=jnp.bfloat16):
    level = block_levels(own_key, shape, cuts, -0.22, 0.18) if cuts else 1.0
    drawn = jax.random.normal(own_key, shape, jnp.float32) * deviation * level
    return jnp.minimum(jnp.maximum(drawn, -bound), bound).astype(held_as)


def setup_inputs(seed: int = 0, part: int = 0) -> dict:
    seeds = jax.random.split(jax.random.key(seed), 15)
    part_splits = jax.random.split(jax.random.fold_in(seeds[14], part), 15)
    x_in = scatter_about(part_splits[0], (MB, ROWS, D), 1.0, 6.0, ((1, 16),))
    queries = draw_queries(jax.random.fold_in(jax.random.fold_in(seeds[14], part), 71), part)
    cache_keys = draw_cache_keys(jax.random.fold_in(jax.random.fold_in(seeds[14], part), 71), part)
    cache_values = scatter_about(part_splits[3], (MB, ROWS, LEN, KVH * HD), 1.0, 6.0, ((1, 16),))
    new_keys = scatter_about(part_splits[4], (MB, ROWS, KVH * HD), 1.0, 6.0, ((1, 16),))
    new_values = scatter_about(part_splits[5], (MB, ROWS, KVH * HD), 1.0, 6.0, ((1, 16),))
    lengths = set_ends(jax.random.randint(part_splits[6], (MB, ROWS), 1, LEN + 1), jax.random.fold_in(part_splits[6], 1), 1, LEN).astype(jnp.int32)
    w_out = scatter_about(seeds[7], (QH * HD, D), (QH * HD) ** -0.5, 0.109375, ((0, 16),))
    norm_gain = jnp.clip(1.0 + 0.15 * jax.random.normal(seeds[8], (D,), jnp.float32), 0.25, 1.75).astype(jnp.bfloat16)
    w_router = scatter_about(seeds[9], (D, E), (D // 9) ** -0.5, 0.3125)
    experts_idx_keys = jax.random.split(jax.random.fold_in(part_splits[10], 1), MB * ROWS // S_DEV)
    experts_idx_turns = jax.random.permutation(jax.random.fold_in(part_splits[10], 3), MB * ROWS // S_DEV)
    experts_idx = jax.vmap(lambda own, number: deal_out(jax.random.fold_in(part_splits[10], 2), own, number, S_DEV, E, 2, S_DEV, 2))(experts_idx_keys, experts_idx_turns).reshape((MB, ROWS, TOPK))
    w_gate = scatter_about(seeds[11], (D, E * FF), D ** -0.5, 0.109375, ((1, 16),))
    w_up = scatter_about(seeds[12], (D, E * FF), D ** -0.5, 0.109375, ((1, 16),))
    w_down = scatter_about(seeds[13], (E * FF, D), FF ** -0.5, 0.0625, ((0, 16),))
    return dict(x_in=x_in, queries=queries, cache_keys=cache_keys, cache_values=cache_values, new_keys=new_keys, new_values=new_values, lengths=lengths, w_out=w_out, norm_gain=norm_gain, w_router=w_router, experts_idx=experts_idx, w_gate=w_gate, w_up=w_up, w_down=w_down)


def attend(query, keys_cache, values_cache, key_new, value_new, length):
    row_count = query.shape[0]
    cache_len = keys_cache.shape[1]
    q_heads = query.astype(jnp.float32).reshape(row_count, KVH, QH // KVH, HD)
    k_heads = keys_cache.astype(jnp.float32).reshape(row_count, cache_len, KVH, HD)
    v_heads = values_cache.astype(jnp.float32).reshape(row_count, cache_len, KVH, HD)
    k_own = key_new.astype(jnp.float32).reshape(row_count, KVH, HD)
    v_own = value_new.astype(jnp.float32).reshape(row_count, KVH, 1, HD)
    score_scale = 1.0 / HD ** 0.5
    scores = jnp.einsum('rkgd,rlkd->rkgl', q_heads, k_heads, precision=lax.Precision.HIGHEST) * score_scale
    own_score = jnp.einsum('rkgd,rkd->rkg', q_heads, k_own, precision=lax.Precision.HIGHEST) * score_scale
    live_mask = (jnp.arange(cache_len)[None, :] < length[:, None])[:, None, None, :]
    peak = jnp.maximum(lax.optimization_barrier(jnp.max(jnp.where(live_mask, scores, -jnp.inf), axis=-1)), own_score)
    weights_cache = jnp.where(live_mask, jnp.exp(scores - peak[..., None]), 0.0)
    weight_own = jnp.exp(own_score - peak)
    total_mass = lax.optimization_barrier(jnp.sum(weights_cache, axis=-1)) + weight_own
    probs = (weights_cache / total_mass[..., None]).astype(jnp.bfloat16)
    prob_own = (weight_own / total_mass).astype(jnp.bfloat16)
    mixed_cache = jnp.einsum('rkgl,rlkd->rkgd', probs.astype(jnp.float32), v_heads, precision=lax.Precision.HIGHEST)
    mixed_own = prob_own.astype(jnp.float32)[..., None] * v_own
    return (mixed_cache + mixed_own).reshape(row_count, QH * HD).astype(jnp.bfloat16)

def reference(x_in, queries, cache_keys, cache_values, new_keys, new_values, lengths, w_out, norm_gain, w_router, experts_idx, w_gate, w_up, w_down):
    results = []
    for micro in range(MB):
        attention = attend(queries[micro], cache_keys[micro], cache_values[micro], new_keys[micro], new_values[micro], lengths[micro])
        attn_out = jnp.dot(attention, w_out, preferred_element_type=jnp.float32)
        resid = x_in[micro].astype(jnp.float32) + attn_out
        mean_square = lax.optimization_barrier(jnp.mean(resid * resid, axis=-1, keepdims=True))
        normed = (resid * lax.rsqrt(mean_square + 1e-05) * norm_gain.astype(jnp.float32)).astype(jnp.bfloat16)
        logits = jnp.dot(normed, w_router, preferred_element_type=jnp.float32)
        route_ids = experts_idx[micro]
        chosen = jnp.take_along_axis(logits, route_ids, axis=-1)
        combine = jax.nn.softmax(chosen, axis=-1)
        moe_total = jnp.zeros(resid.shape, jnp.float32)
        for expert in range(E):
            expert_weight = lax.optimization_barrier(jnp.sum(jnp.where(route_ids == expert, combine, 0.0), axis=-1))
            gate = jnp.dot(normed, w_gate[:, expert * FF:(expert + 1) * FF], preferred_element_type=jnp.float32)
            upper = jnp.dot(normed, w_up[:, expert * FF:(expert + 1) * FF], preferred_element_type=jnp.float32)
            hidden = (jax.nn.silu(gate) * upper).astype(jnp.bfloat16)
            expert_out = jnp.dot(hidden, w_down[expert * FF:(expert + 1) * FF], preferred_element_type=jnp.float32)
            moe_total = moe_total + expert_weight[:, None] * expert_out
        results.append((resid + moe_total).astype(jnp.bfloat16))
    return jnp.stack(results)
```

```python
import math

import jax
import jax.numpy as jnp
from jax import lax
from jax.sharding import PartitionSpec as P

QH = 24
KVH = 4
HD = 128


def attend_rows(query, keys_cache, values_cache, key_new, value_new, length):
    row_count = keys_cache.shape[0]
    cache_len = keys_cache.shape[1]
    q_heads = query.reshape(row_count, KVH, QH // KVH, HD)
    k_heads = keys_cache.reshape(row_count, cache_len, KVH, HD)
    v_heads = values_cache.reshape(row_count, cache_len, KVH, HD)
    score_scale = 1.0 / math.sqrt(HD)
    scores = (
        jnp.einsum("rkgd,rlkd->rkgl", q_heads, k_heads, preferred_element_type=jnp.float32)
        * score_scale
    )
    own_score = (
        jnp.einsum(
            "rkgd,rkd->rkg",
            q_heads,
            key_new.reshape(row_count, KVH, HD),
            preferred_element_type=jnp.float32,
        )
        * score_scale
    )
    live_mask = (jnp.arange(cache_len)[None, :] < length[:, None])[:, None, None, :]
    peak = jnp.maximum(jnp.max(jnp.where(live_mask, scores, -jnp.inf), axis=-1), own_score)
    weights_cache = jnp.where(live_mask, jnp.exp(scores - peak[..., None]), 0.0)
    weight_own = jnp.exp(own_score - peak)
    total_mass = jnp.sum(weights_cache, axis=-1) + weight_own
    probs = (weights_cache / total_mass[..., None]).astype(jnp.bfloat16)
    prob_own = (weight_own / total_mass).astype(jnp.bfloat16)
    mixed_cache = jnp.einsum("rkgl,rlkd->rkgd", probs, v_heads, preferred_element_type=jnp.float32)
    mixed_own = prob_own.astype(jnp.float32)[..., None] * value_new.reshape(
        row_count, KVH, 1, HD
    ).astype(jnp.float32)
    return (mixed_cache + mixed_own).reshape(row_count, QH * HD).astype(jnp.bfloat16)


def row_weights(normed, route_ids, w_router):
    logits = jnp.dot(normed, w_router, preferred_element_type=jnp.float32)
    expert_count = w_router.shape[1]
    member_of = (route_ids[:, :, None] == jnp.arange(expert_count)[None, None, :]).astype(
        jnp.float32
    )
    chosen = jnp.sum(member_of * logits[:, None, :], axis=-1)
    combine = jax.nn.softmax(chosen, axis=-1)
    return jnp.sum(member_of * combine[:, :, None], axis=1)


def exchange(blocks):
    return lax.all_to_all(blocks, "dev", split_axis=0, concat_axis=0, tiled=True)


def local(
    x_in,
    queries,
    cache_keys,
    cache_values,
    new_keys,
    new_values,
    lengths,
    w_out,
    norm_gain,
    w_router,
    experts_idx,
    w_gate,
    w_up,
    w_down,
):
    devices = lax.axis_size("dev")
    expert_count = w_router.shape[1]
    per_expert = devices // expert_count
    out_shape = x_in.shape
    feature_dim = out_shape[2]
    rows = out_shape[0] * out_shape[1]

    def flat(a):
        return a.reshape((rows,) + a.shape[2:])

    attention = attend_rows(
        flat(queries),
        flat(cache_keys),
        flat(cache_values),
        flat(new_keys),
        flat(new_values),
        flat(lengths),
    )
    heads = jnp.transpose(attention.reshape(rows, devices, -1), (1, 0, 2))
    head_block = exchange(heads).reshape(devices * rows, -1)
    partial_attn = jnp.dot(head_block, w_out, preferred_element_type=jnp.float32)
    attn_parts = exchange(partial_attn.astype(jnp.bfloat16).reshape(devices, rows, feature_dim))
    resid = flat(x_in).astype(jnp.float32) + jnp.sum(attn_parts.astype(jnp.float32), axis=0)
    mean_square = jnp.mean(resid * resid, axis=-1, keepdims=True)
    normed = (resid * lax.rsqrt(mean_square + 1e-05) * norm_gain.astype(jnp.float32)).astype(
        jnp.bfloat16
    )
    weights = row_weights(normed, flat(experts_idx), w_router)
    high = weights.astype(jnp.bfloat16)
    low = (weights - high.astype(jnp.float32)).astype(jnp.bfloat16)
    padding = jnp.zeros((rows, 128 - 2 * expert_count), jnp.bfloat16)
    message = jnp.concatenate([normed, high, low, padding], axis=1)
    received = exchange(jnp.broadcast_to(message[None], (devices,) + message.shape))
    received = received.reshape(devices * rows, -1)
    all_rows = received[:, :feature_dim]
    packed = received[:, feature_dim : feature_dim + 2 * expert_count].astype(jnp.float32)
    expert = lax.axis_index("dev") // per_expert
    mine = (jnp.arange(2 * expert_count) % expert_count == expert).astype(jnp.float32)
    my_weight = jnp.sum(packed * mine[None, :], axis=1, keepdims=True)
    gate = jnp.dot(all_rows, w_gate, preferred_element_type=jnp.float32)
    upper = jnp.dot(all_rows, w_up, preferred_element_type=jnp.float32)
    hidden = (jax.nn.silu(gate) * upper).astype(jnp.bfloat16)
    partial = jnp.dot(hidden, w_down, preferred_element_type=jnp.float32) * my_weight
    parts = exchange(partial.astype(jnp.bfloat16).reshape(devices, rows, feature_dim))
    mixed = resid + jnp.sum(parts.astype(jnp.float32), axis=0)
    return mixed.astype(jnp.bfloat16).reshape(out_shape)


def solution(mesh):
    return jax.shard_map(
        local,
        mesh=mesh,
        in_specs=(
            P(None, ("groups", "dev"), None),
            P(None, ("groups", "dev"), None),
            P(None, ("groups", "dev"), None, None),
            P(None, ("groups", "dev"), None, None),
            P(None, ("groups", "dev"), None),
            P(None, ("groups", "dev"), None),
            P(None, ("groups", "dev")),
            P("dev", None),
            P(),
            P(),
            P(None, ("groups", "dev"), None),
            P(None, "dev"),
            P(None, "dev"),
            P("dev", None),
        ),
        out_specs=P(None, ("groups", "dev"), None),
        check_vma=False,
    )
```

```python
import math

import jax
import jax.numpy as jnp
from jax import lax
from jax.experimental import pallas as pl
from jax.experimental.pallas import tpu as pltpu
from jax.sharding import PartitionSpec as P

QH = 24
KVH = 4
HD = 128
LANES = 128
MIB = 1 << 20

VMEM = pl.BlockSpec(memory_space=pltpu.VMEM)
SMEM = pl.BlockSpec(memory_space=pltpu.SMEM)


def params(mib):
    return pltpu.CompilerParams(vmem_limit_bytes=mib * MIB)


def attend_kernel(len_ref, q_ref, k_ref, v_ref, nk_ref, nv_ref, out_ref):
    batches, sessions = q_ref.shape[:2]
    cache_len = k_ref.shape[2]
    width = KVH * HD
    per_kv = QH // KVH
    scale = 1.0 / math.sqrt(HD)
    head = lax.broadcasted_iota(jnp.int32, (QH, width), 0) // per_kv
    lane = lax.broadcasted_iota(jnp.int32, (QH, width), 1) // HD
    own_kv = head == lane
    slot = lax.broadcasted_iota(jnp.int32, (QH, cache_len), 1)
    rows = []
    for m in range(batches):
        q_all = q_ref[m].astype(jnp.float32)
        nk_all = nk_ref[m].astype(jnp.float32)
        nv_all = nv_ref[m].astype(jnp.float32)
        for s in range(sessions):
            q_row = q_all[s : s + 1]
            q_heads = jnp.concatenate([q_row[:, h * HD : (h + 1) * HD] for h in range(QH)], axis=0)
            q_wide = jnp.where(own_kv, jnp.concatenate([q_heads] * KVH, axis=1), 0.0)
            scores = (
                lax.dot_general(
                    q_wide.astype(jnp.bfloat16),
                    k_ref[m, s],
                    (((1,), (1,)), ((), ())),
                    preferred_element_type=jnp.float32,
                )
                * scale
            )
            own_score = jnp.sum(q_wide * nk_all[s : s + 1], axis=1, keepdims=True) * scale
            live = slot < len_ref[m, s]
            peak = jnp.maximum(
                jnp.max(jnp.where(live, scores, -jnp.inf), axis=1, keepdims=True), own_score
            )
            mass = jnp.where(live, jnp.exp(scores - peak), 0.0)
            own_mass = jnp.exp(own_score - peak)
            total = jnp.sum(mass, axis=1, keepdims=True) + own_mass
            probs = (mass / total).astype(jnp.bfloat16)
            own_prob = (own_mass / total).astype(jnp.bfloat16).astype(jnp.float32)
            wide = jnp.dot(probs, v_ref[m, s], preferred_element_type=jnp.float32)
            wide = jnp.where(own_kv, wide + own_prob * nv_all[s : s + 1], 0.0)
            heads = wide[:, :HD]
            for k in range(1, KVH):
                heads = heads + wide[:, k * HD : (k + 1) * HD]
            rows.append(jnp.concatenate([heads[h : h + 1] for h in range(QH)], axis=1))
    attention = jnp.concatenate(rows, axis=0).astype(jnp.bfloat16)
    devices, _, part = out_ref.shape
    for d in range(devices):
        out_ref[d] = attention[:, d * part : (d + 1) * part]


def stacked(ref, width):
    blocks = [ref[d][:, :width].astype(jnp.float32) for d in range(ref.shape[0])]
    return jnp.concatenate(blocks, axis=0).astype(jnp.bfloat16)


def project_kernel(x_ref, w_ref, out_ref):
    devices, rows, features = out_ref.shape
    inputs = stacked(x_ref, x_ref.shape[2])
    chunk = 512 if features % 512 == 0 else LANES
    for start in range(0, features, chunk):
        part = jnp.dot(
            inputs, w_ref[:, start : start + chunk], preferred_element_type=jnp.float32
        )
        for d in range(devices):
            out_ref[d, :, start : start + chunk] = part[d * rows : (d + 1) * rows].astype(
                jnp.bfloat16
            )


def norm_kernel(idx_ref, parts_ref, x_ref, gain_ref, router_ref, resid_ref, out_ref):
    batches, sessions, features = x_ref.shape
    experts = router_ref.shape[1]
    rows = batches * sessions
    x_rows = jnp.concatenate([x_ref[m].astype(jnp.float32) for m in range(batches)], axis=0)
    total = parts_ref[0].astype(jnp.float32)
    for d in range(1, parts_ref.shape[0]):
        total = total + parts_ref[d].astype(jnp.float32)
    resid = x_rows + total
    resid_ref[...] = resid
    mean_square = jnp.mean(resid * resid, axis=1, keepdims=True)
    normed = (resid * lax.rsqrt(mean_square + 1e-05) * gain_ref[...].astype(jnp.float32)).astype(
        jnp.bfloat16
    )
    logits = jnp.dot(normed, router_ref[...], preferred_element_type=jnp.float32)
    row = lax.broadcasted_iota(jnp.int32, (rows, experts), 0)
    column = lax.broadcasted_iota(jnp.int32, (rows, experts), 1)
    member = row < 0
    for m in range(batches):
        for s in range(sessions):
            for k in range(idx_ref.shape[2]):
                member = member | ((row == m * sessions + s) & (column == idx_ref[m, s, k]))
    peak = jnp.max(jnp.where(member, logits, -jnp.inf), axis=1, keepdims=True)
    mass = jnp.where(member, jnp.exp(logits - peak), 0.0)
    weights = mass / jnp.sum(mass, axis=1, keepdims=True)
    high = weights.astype(jnp.bfloat16).astype(jnp.float32)
    low = weights - high
    extra = jnp.concatenate(
        [high, low, jnp.zeros((rows, LANES - 2 * experts), jnp.float32)], axis=1
    ).astype(jnp.bfloat16)
    for d in range(out_ref.shape[0]):
        out_ref[d, :, :features] = normed
        out_ref[d, :, features:] = extra


def expert_kernel(expert_count, expert_ref, x_ref, gate_ref, up_ref, down_ref, out_ref, hidden):
    devices, rows, features = out_ref.shape
    units = gate_ref.shape[1]
    inputs = stacked(x_ref, features)
    packed = jnp.concatenate(
        [x_ref[d][:, features:].astype(jnp.float32) for d in range(devices)], axis=0
    )
    lane = lax.broadcasted_iota(jnp.int32, packed.shape, 1)
    mine = (lane % expert_count == expert_ref[0]) & (lane < 2 * expert_count)
    weight = jnp.sum(jnp.where(mine, packed, 0.0), axis=1, keepdims=True)
    chunk = min(512, units)
    for start in range(0, units, chunk):
        cut = slice(start, start + chunk)
        gate = jnp.dot(inputs, gate_ref[:, cut], preferred_element_type=jnp.float32)
        upper = jnp.dot(inputs, up_ref[:, cut], preferred_element_type=jnp.float32)
        hidden[:, cut] = (jax.nn.silu(gate) * upper).astype(jnp.bfloat16)
    chunk = 512 if features % 512 == 0 else LANES
    for start in range(0, features, chunk):
        cut = slice(start, start + chunk)
        part = jnp.dot(hidden[...], down_ref[:, cut], preferred_element_type=jnp.float32) * weight
        for d in range(devices):
            out_ref[d, :, cut] = part[d * rows : (d + 1) * rows].astype(jnp.bfloat16)


def final_kernel(resid_ref, parts_ref, out_ref):
    batches, sessions, _ = out_ref.shape
    total = parts_ref[0].astype(jnp.float32)
    for d in range(1, parts_ref.shape[0]):
        total = total + parts_ref[d].astype(jnp.float32)
    mixed = resid_ref[...] + total
    for m in range(batches):
        out_ref[m] = mixed[m * sessions : (m + 1) * sessions].astype(jnp.bfloat16)


def exchange(blocks):
    return lax.all_to_all(blocks, "dev", split_axis=0, concat_axis=0, tiled=True)


def local(
    x_in,
    queries,
    cache_keys,
    cache_values,
    new_keys,
    new_values,
    lengths,
    w_out,
    norm_gain,
    w_router,
    experts_idx,
    w_gate,
    w_up,
    w_down,
):
    devices = lax.axis_size("dev")
    expert_count = w_router.shape[1]
    batches, sessions, features = x_in.shape
    rows = batches * sessions
    units = w_gate.shape[1]

    def blocks(width):
        return jax.ShapeDtypeStruct((devices, rows, width), jnp.bfloat16)

    heads = pl.pallas_call(
        attend_kernel,
        in_specs=[SMEM] + [VMEM] * 5,
        out_specs=VMEM,
        out_shape=blocks(w_out.shape[0]),
        compiler_params=params(8),
        name="attend",
    )(lengths, queries, cache_keys, cache_values, new_keys, new_values)
    head_blocks = exchange(heads)
    partial_attn = pl.pallas_call(
        project_kernel,
        in_specs=[VMEM] * 2,
        out_specs=VMEM,
        out_shape=blocks(features),
        compiler_params=params(8),
        name="project",
    )(head_blocks, w_out)
    attn_parts = exchange(partial_attn)
    resid, message = pl.pallas_call(
        norm_kernel,
        in_specs=[SMEM] + [VMEM] * 4,
        out_specs=(VMEM, VMEM),
        out_shape=(jax.ShapeDtypeStruct((rows, features), jnp.float32), blocks(features + LANES)),
        compiler_params=params(8),
        name="norm",
    )(experts_idx, attn_parts, x_in, norm_gain.reshape(1, features), w_router)
    received = exchange(message)
    expert = (lax.axis_index("dev") // (devices // expert_count)).astype(jnp.int32)
    partial = pl.pallas_call(
        lambda *refs: expert_kernel(expert_count, *refs),
        in_specs=[SMEM] + [VMEM] * 4,
        out_specs=VMEM,
        out_shape=blocks(features),
        scratch_shapes=[pltpu.VMEM((devices * rows, units), jnp.bfloat16)],
        compiler_params=params(8),
        name="experts",
    )(
        expert.reshape(1),
        received,
        *[pltpu.with_memory_space_constraint(w, pltpu.VMEM) for w in (w_gate, w_up, w_down)],
    )
    parts = exchange(partial)
    return pl.pallas_call(
        final_kernel,
        in_specs=[VMEM] * 2,
        out_specs=VMEM,
        out_shape=jax.ShapeDtypeStruct(x_in.shape, jnp.bfloat16),
        compiler_params=params(8),
        name="final",
    )(resid, parts)


def solution(mesh):
    return jax.shard_map(
        local,
        mesh=mesh,
        in_specs=(
            P(None, ("groups", "dev"), None),
            P(None, ("groups", "dev"), None),
            P(None, ("groups", "dev"), None, None),
            P(None, ("groups", "dev"), None, None),
            P(None, ("groups", "dev"), None),
            P(None, ("groups", "dev"), None),
            P(None, ("groups", "dev")),
            P("dev", None),
            P(),
            P(),
            P(None, ("groups", "dev"), None),
            P(None, "dev"),
            P(None, "dev"),
            P("dev", None),
        ),
        out_specs=P(None, ("groups", "dev"), None),
        check_vma=False,
    )
```

```python
import math

import jax
import jax.numpy as jnp
from jax import lax
from jax.experimental import pallas as pl
from jax.experimental.pallas import tpu as pltpu
from jax.sharding import PartitionSpec as P

QH = 24
KVH = 4
HD = 128
LANES = 128
CHUNK = 512
MIB = 1 << 20

VMEM = pl.BlockSpec(memory_space=pltpu.VMEM)
SMEM = pl.BlockSpec(memory_space=pltpu.SMEM)
HBM = pl.BlockSpec(memory_space=pltpu.HBM)
ANY = pl.BlockSpec(memory_space=pl.ANY)


def params(mib):
    return pltpu.CompilerParams(vmem_limit_bytes=mib * MIB)


def attend_kernel(len_ref, *refs):
    operands, out_ref, buffers, sems = refs[:5], refs[5], refs[6:11], refs[11]
    copies = [
        pltpu.make_async_copy(operands[i], buffers[i], sems.at[i])
        for i in range(len(operands))
    ]
    for copy in copies:
        copy.start()
    for copy in copies:
        copy.wait()
    q_ref, k_ref, v_ref, nk_ref, nv_ref = buffers
    batches, sessions = q_ref.shape[:2]
    cache_len = k_ref.shape[2]
    width = KVH * HD
    per_kv = QH // KVH
    scale = 1.0 / math.sqrt(HD)
    head = lax.broadcasted_iota(jnp.int32, (QH, width), 0) // per_kv
    lane = lax.broadcasted_iota(jnp.int32, (QH, width), 1) // HD
    own_kv = head == lane
    slot = lax.broadcasted_iota(jnp.int32, (QH, cache_len), 1)
    rows = []
    for m in range(batches):
        q_all = q_ref[m].astype(jnp.float32)
        nk_all = nk_ref[m].astype(jnp.float32)
        nv_all = nv_ref[m].astype(jnp.float32)
        for s in range(sessions):
            q_row = q_all[s : s + 1]
            q_heads = jnp.concatenate([q_row[:, h * HD : (h + 1) * HD] for h in range(QH)], axis=0)
            q_wide = jnp.where(own_kv, jnp.concatenate([q_heads] * KVH, axis=1), 0.0)
            scores = (
                lax.dot_general(
                    q_wide.astype(jnp.bfloat16),
                    k_ref[m, s],
                    (((1,), (1,)), ((), ())),
                    preferred_element_type=jnp.float32,
                )
                * scale
            )
            own_score = jnp.sum(q_wide * nk_all[s : s + 1], axis=1, keepdims=True) * scale
            live = slot < len_ref[m, s]
            peak = jnp.maximum(
                jnp.max(jnp.where(live, scores, -jnp.inf), axis=1, keepdims=True), own_score
            )
            mass = jnp.where(live, jnp.exp(scores - peak), 0.0)
            own_mass = jnp.exp(own_score - peak)
            total = jnp.sum(mass, axis=1, keepdims=True) + own_mass
            probs = (mass / total).astype(jnp.bfloat16)
            own_prob = (own_mass / total).astype(jnp.bfloat16).astype(jnp.float32)
            wide = jnp.dot(probs, v_ref[m, s], preferred_element_type=jnp.float32)
            wide = jnp.where(own_kv, wide + own_prob * nv_all[s : s + 1], 0.0)
            heads = wide[:, :HD]
            for k in range(1, KVH):
                heads = heads + wide[:, k * HD : (k + 1) * HD]
            rows.append(jnp.concatenate([heads[h : h + 1] for h in range(QH)], axis=1))
    attention = jnp.concatenate(rows, axis=0).astype(jnp.bfloat16)
    devices, _, part = out_ref.shape
    for d in range(devices):
        out_ref[d] = attention[:, d * part : (d + 1) * part]


PIECES = 4


def fetch_kernel(cuts, *refs):
    count = len(cuts)
    sources, targets, token, sems = refs[:count], refs[-count - 2 : -2], refs[-2], refs[-1]
    token[...] = jnp.zeros(token.shape, token.dtype)
    copies = []
    for source, target, cut in zip(sources, targets, cuts):
        if cut is None:
            copies.append(pltpu.make_async_copy(source, target, sems.at[len(copies)]))
        else:
            size = cut[1] // PIECES
            for at in range(0, cut[1], size):
                copies.append(
                    pltpu.make_async_copy(
                        source.at[pl.ds(cut[0] + at, size)],
                        target.at[pl.ds(at, size)],
                        sems.at[len(copies)],
                    )
                )
    for copy in copies:
        copy.start()
    for copy in copies:
        copy.wait()


def fetch(arrays, cuts, after, name):
    shapes = [a.shape if c is None else (c[1],) + a.shape[1:] for a, c in zip(arrays, cuts)]
    total = 2 * sum(math.prod(shape) for shape in shapes)
    copies = sum(1 if c is None else PIECES for c in cuts)
    return pl.pallas_call(
        lambda *refs: fetch_kernel(cuts, *refs),
        in_specs=[HBM] * len(arrays) + [ANY],
        out_specs=[VMEM] * (len(arrays) + 1),
        out_shape=[pltpu.VMEM(shape, a.dtype) for shape, a in zip(shapes, arrays)]
        + [jax.ShapeDtypeStruct((8, LANES), jnp.float32)],
        scratch_shapes=[pltpu.SemaphoreType.DMA((copies,))],
        compiler_params=params(8),
        cost_estimate=pl.CostEstimate(flops=0, bytes_accessed=total, transcendentals=0),
        name=name,
    )(*[far(a) for a in arrays], after)


def far(array):
    return pltpu.with_memory_space_constraint(array, pltpu.HBM)


def here(array):
    return pltpu.with_memory_space_constraint(array, pltpu.VMEM)


def rows_of(ref, order):
    blocks = [ref[d].astype(jnp.float32) for d in order]
    return jnp.concatenate(blocks, axis=0)


def send_blocks(refs, value, cut, rows):
    at = 0
    for ref in refs:
        for k in range(ref.shape[0]):
            ref[k, :, cut] = value[at : at + rows].astype(ref.dtype)
            at += rows


def project_kernel(order, x_ref, w_ref, *out_refs):
    rows, features = out_refs[0].shape[1:]
    me = lax.axis_index("dev")
    inputs = rows_of(x_ref, [me ^ k for k in order]).astype(jnp.bfloat16)
    for start in range(0, features, CHUNK):
        cut = slice(start, start + CHUNK)
        part = jnp.dot(inputs, w_ref[:, cut], preferred_element_type=jnp.float32)
        send_blocks(out_refs, part, cut, rows)


def total_of(refs):
    total = refs[0][...].astype(jnp.float32)
    for ref in refs[1:]:
        total = total + ref[...].astype(jnp.float32)
    return total


def fold_kernel(count, outs, *refs):
    total = total_of(refs[:count])
    at = 0
    for ref in refs[-outs:]:
        ref[...] = total[at : at + ref.shape[0]].astype(ref.dtype)
        at += ref.shape[0]


def fold(parts, outs, idle):
    blocks, rows, features = parts[0].shape
    shape = (blocks // outs, rows, features)
    return pl.pallas_call(
        lambda *refs: fold_kernel(len(parts), outs, *refs),
        in_specs=[VMEM] * len(parts) + [HBM] * len(idle),
        out_specs=[VMEM] * outs,
        out_shape=[jax.ShapeDtypeStruct(shape, jnp.float32)]
        + [jax.ShapeDtypeStruct(shape, jnp.bfloat16)] * (outs - 1),
        compiler_params=params(8),
        name="fold",
    )(*parts, *[far(a) for a in idle])


def norm_kernel(idx_ref, x_ref, gain_ref, router_ref, *refs):
    resid_ref, out_ref = refs[-2:]
    batches, sessions, features = x_ref.shape
    experts = router_ref.shape[0]
    rows = batches * sessions
    x_rows = jnp.concatenate([x_ref[m].astype(jnp.float32) for m in range(batches)], axis=0)
    resid = x_rows + total_of(refs[:-2])[0]
    resid_ref[...] = resid
    mean_square = jnp.mean(resid * resid, axis=1, keepdims=True)
    normed = (resid * lax.rsqrt(mean_square + 1e-05) * gain_ref[...].astype(jnp.float32).reshape(1, features)).astype(
        jnp.bfloat16
    )
    logits = lax.dot_general(
        normed, router_ref[...], (((1,), (1,)), ((), ())), preferred_element_type=jnp.float32
    )
    row = lax.broadcasted_iota(jnp.int32, (rows, experts), 0)
    column = lax.broadcasted_iota(jnp.int32, (rows, experts), 1)
    member = row < 0
    for m in range(batches):
        for s in range(sessions):
            for k in range(idx_ref.shape[2]):
                member = member | ((row == m * sessions + s) & (column == idx_ref[m, s, k]))
    peak = jnp.max(jnp.where(member, logits, -jnp.inf), axis=1, keepdims=True)
    mass = jnp.where(member, jnp.exp(logits - peak), 0.0)
    weights = mass / jnp.sum(mass, axis=1, keepdims=True)
    high = weights.astype(jnp.bfloat16).astype(jnp.float32)
    low = weights - high
    extra = jnp.concatenate(
        [high, low, jnp.zeros((rows, LANES - 2 * experts), jnp.float32)], axis=1
    ).astype(jnp.bfloat16)
    out_ref[0, :, :features] = normed
    out_ref[0, :, features:] = extra


def expert_kernel(expert_count, near_ref, far_ref, gate, up, down, *refs):
    out_refs, hidden = refs[:-1], refs[-1]
    rows, features = out_refs[0].shape[1:]
    units = hidden.shape[1]
    near, other = [[ref[d].astype(jnp.float32) for d in range(ref.shape[0])] for ref in (near_ref, far_ref)]
    blocks = near + other
    order, kept = scatter_order(len(blocks)), gather_order(len(blocks))
    whole = jnp.concatenate([blocks[kept.index(k)] for k in order], axis=0)
    inputs = whole[:, :features].astype(jnp.bfloat16)
    packed = whole[:, features:]
    expert = lax.div(lax.axis_index("dev"), len(blocks) // expert_count)
    lane = lax.broadcasted_iota(jnp.int32, packed.shape, 1)
    mine = (lane % expert_count == expert) & (lane < 2 * expert_count)
    weight = jnp.sum(jnp.where(mine, packed, 0.0), axis=1, keepdims=True)

    def product(weights, cut):
        return jnp.dot(inputs, weights[:, cut], preferred_element_type=jnp.float32)

    for start in range(0, units, CHUNK):
        cut = slice(start, start + CHUNK)
        hidden[:, cut] = (jax.nn.silu(product(gate, cut)) * product(up, cut)).astype(jnp.bfloat16)
    for start in range(0, features, CHUNK):
        cut = slice(start, start + CHUNK)
        part = jnp.dot(hidden[...], down[:, cut], preferred_element_type=jnp.float32)
        send_blocks(out_refs, part * weight, cut, rows)


def stages_of(devices):
    stages, bit = [], 2
    while bit < devices:
        if bit > 2 and 2 * bit < devices:
            stages.append((bit, 2 * bit, 3 * bit))
            bit *= 4
        else:
            stages.append((bit,))
            bit *= 2
    return stages


def gather_order(devices):
    order = [0]
    for masks in stages_of(devices):
        order = order + [mask ^ k for mask in masks for k in order]
    return order + [1 ^ k for k in order]


def scatter_order(devices):
    order = [0]
    for masks in reversed([(1,)] + stages_of(devices)):
        order = order + [mask ^ k for mask in masks for k in order]
    return order


def hop(blocks, mask):
    devices = lax.axis_size("dev")
    return lax.ppermute(blocks, "dev", [(i, i ^ mask) for i in range(devices)])


def gather(block, idle):
    for masks in stages_of(lax.axis_size("dev")):
        block = join([block] + [hop(block, mask) for mask in masks], idle)
    return block, hop(block, 1)


def join_kernel(count, *refs):
    size = refs[0].shape[0]
    for k in range(count):
        refs[-1][k * size : (k + 1) * size] = refs[k][...]


def join(parts, idle):
    shape = (len(parts) * parts[0].shape[0],) + parts[0].shape[1:]
    return pl.pallas_call(
        lambda *refs: join_kernel(len(parts), *refs),
        in_specs=[VMEM] * len(parts) + [HBM] * len(idle),
        out_specs=VMEM,
        out_shape=jax.ShapeDtypeStruct(shape, parts[0].dtype),
        compiler_params=params(8),
        name="join",
    )(*parts, *[far(a) for a in idle])


def scatter(keep, sends, idle):
    stages = [(1,)] + stages_of(lax.axis_size("dev"))
    for step, masks in enumerate(stages):
        parts = [keep] + [hop(block, mask) for block, mask in zip(sends, masks)]
        if step + 1 < len(stages):
            keep, *sends = fold(parts, len(stages[step + 1]) + 1, idle)
    return parts


def final_kernel(*refs):
    resid_ref, out_ref = refs[0], refs[-1]
    batches, sessions, _ = out_ref.shape
    mixed = resid_ref[...] + total_of(refs[1:-1])[0]
    for m in range(batches):
        out_ref[m] = mixed[m * sessions : (m + 1) * sessions].astype(jnp.bfloat16)


def exchange(blocks):
    return lax.all_to_all(blocks, "dev", split_axis=0, concat_axis=0, tiled=True)


def local(
    x_in,
    queries,
    cache_keys,
    cache_values,
    new_keys,
    new_values,
    lengths,
    w_out,
    norm_gain,
    w_router,
    experts_idx,
    w_gate,
    w_up,
    w_down,
):
    devices = lax.axis_size("dev")
    expert_count = w_router.shape[1]
    batches, sessions, features = x_in.shape
    rows = batches * sessions
    units = w_gate.shape[1]

    def blocks(width):
        return jax.ShapeDtypeStruct((devices, rows, width), jnp.bfloat16)

    operands = [queries, cache_keys, cache_values, new_keys, new_values]
    heads = pl.pallas_call(
        attend_kernel,
        in_specs=[SMEM] + [HBM] * 5,
        out_specs=VMEM,
        out_shape=blocks(w_out.shape[0]),
        scratch_shapes=[pltpu.VMEM(a.shape, a.dtype) for a in operands]
        + [pltpu.SemaphoreType.DMA((len(operands),))],
        compiler_params=params(8),
        name="attend",
    )(lengths, *[pltpu.with_memory_space_constraint(a, pltpu.HBM) for a in operands])
    head_blocks = exchange(heads)
    (out_here, _) = fetch([w_out], [None], heads, "fetch_out")
    halves = [jax.ShapeDtypeStruct((devices // 2, rows, features), t) for t in (jnp.float32, jnp.bfloat16)]
    keep, send = pl.pallas_call(
        lambda *refs: project_kernel(scatter_order(devices), *refs),
        in_specs=[VMEM] * 2,
        out_specs=[VMEM] * 2,
        out_shape=halves,
        compiler_params=params(8),
        name="project",
    )(head_blocks, here(out_here))
    attn_parts = scatter(keep, [send], [w_gate])
    resid, message = pl.pallas_call(
        norm_kernel,
        in_specs=[SMEM] + [VMEM] * (3 + len(attn_parts)),
        out_specs=(VMEM, VMEM),
        out_shape=(
            pltpu.VMEM((rows, features), jnp.float32),
            jax.ShapeDtypeStruct((1, rows, features + LANES), jnp.bfloat16),
        ),
        compiler_params=params(8),
        name="norm",
    )(experts_idx, here(x_in), norm_gain, jnp.transpose(w_router), *attn_parts)
    near, other = gather(message, [w_gate])
    keep, send = pl.pallas_call(
        lambda *refs: expert_kernel(expert_count, *refs),
        in_specs=[VMEM] * 5,
        out_specs=[VMEM] * 2,
        out_shape=halves,
        scratch_shapes=[
            pltpu.VMEM((devices * rows, units), jnp.bfloat16),
        ],
        compiler_params=params(8),
        name="experts",
    )(near, other, here(w_gate), here(w_up), here(w_down))
    parts = scatter(keep, [send], [])
    return pl.pallas_call(
        final_kernel,
        in_specs=[VMEM] * (1 + len(parts)),
        out_specs=VMEM,
        out_shape=jax.ShapeDtypeStruct(x_in.shape, jnp.bfloat16),
        compiler_params=params(8),
        name="final",
    )(resid, *parts)


def solution(mesh):
    return jax.shard_map(
        local,
        mesh=mesh,
        in_specs=(
            P(None, ("groups", "dev"), None),
            P(None, ("groups", "dev"), None),
            P(None, ("groups", "dev"), None, None),
            P(None, ("groups", "dev"), None, None),
            P(None, ("groups", "dev"), None),
            P(None, ("groups", "dev"), None),
            P(None, ("groups", "dev")),
            P("dev", None),
            P(),
            P(),
            P(None, ("groups", "dev"), None),
            P(None, "dev"),
            P(None, "dev"),
            P("dev", None),
        ),
        out_specs=P(None, ("groups", "dev"), None),
        check_vma=False,
    )
```

```python
import math

import jax
import jax.numpy as jnp
from jax import lax
from jax.experimental import pallas as pl
from jax.experimental.pallas import tpu as pltpu
from jax.sharding import PartitionSpec as P

QH = 24
KVH = 4
HD = 128
LANES = 128
CHUNK = 512
MIB = 1 << 20

VMEM = pl.BlockSpec(memory_space=pltpu.VMEM)
SMEM = pl.BlockSpec(memory_space=pltpu.SMEM)
HBM = pl.BlockSpec(memory_space=pltpu.HBM)
ANY = pl.BlockSpec(memory_space=pl.ANY)


def params(mib):
    return pltpu.CompilerParams(vmem_limit_bytes=mib * MIB)


def attend_kernel(*refs):
    count = (len(refs) - 2) // 2
    operands, out_ref, buffers, sems = refs[:count], refs[count], refs[count + 1 : -1], refs[-1]
    copies = [
        pltpu.make_async_copy(source, target, sems.at[i])
        for i, (source, target) in enumerate(zip(operands, buffers))
    ]
    for copy in copies:
        copy.start()
    for copy in copies:
        copy.wait()
    len_ref, q_ref, nk_ref, k_ref, nv_ref, v_ref = buffers
    batches, sessions = q_ref.shape[:2]
    places = [(m, s) for m in range(batches) for s in range(sessions)]
    cache_len = k_ref.shape[2]
    width = KVH * HD
    per_kv = QH // KVH
    scale = 1.0 / math.sqrt(HD)
    head = lax.broadcasted_iota(jnp.int32, (QH, width), 0) // per_kv
    lane = lax.broadcasted_iota(jnp.int32, (QH, width), 1) // HD
    own_kv = jnp.concatenate([head == lane] * len(places), axis=0)
    slot = lax.broadcasted_iota(jnp.int32, (QH, cache_len), 1)

    def each(piece):
        return jnp.concatenate([piece(m, s) for m, s in places], axis=0)

    def spread(ref):
        full = [ref[m].astype(jnp.float32) for m in range(batches)]
        return each(lambda m, s: jnp.broadcast_to(full[m][s : s + 1], (QH, width)))

    q_all = [q_ref[m].astype(jnp.float32) for m in range(batches)]
    q_heads = jnp.concatenate(
        [q_all[m][s : s + 1, h * HD : (h + 1) * HD] for m, s in places for h in range(QH)], axis=0
    )
    q_wide = jnp.where(own_kv, jnp.concatenate([q_heads] * KVH, axis=1), 0.0)
    q_narrow = q_wide.astype(jnp.bfloat16)
    scores = scale * jnp.concatenate(
        [
            lax.dot_general(
                q_narrow[n * QH : (n + 1) * QH],
                k_ref[m, s],
                (((1,), (1,)), ((), ())),
                preferred_element_type=jnp.float32,
            )
            for n, (m, s) in enumerate(places)
        ],
        axis=0,
    )
    own_score = jnp.sum(q_wide * spread(nk_ref), axis=1, keepdims=True) * scale
    live = each(lambda m, s: slot - len_ref[m, s : s + 1][:, None]) < 0
    peak = jnp.maximum(
        jnp.max(jnp.where(live, scores, -jnp.inf), axis=1, keepdims=True), own_score
    )
    mass = jnp.where(live, jnp.exp(scores - peak), 0.0)
    own_mass = jnp.exp(own_score - peak)
    total = jnp.sum(mass, axis=1, keepdims=True) + own_mass
    probs = (mass / total).astype(jnp.bfloat16)
    own_prob = (own_mass / total).astype(jnp.bfloat16).astype(jnp.float32)
    wide = jnp.concatenate(
        [
            jnp.dot(
                probs[n * QH : (n + 1) * QH], v_ref[m, s], preferred_element_type=jnp.float32
            )
            for n, (m, s) in enumerate(places)
        ],
        axis=0,
    )
    wide = jnp.where(own_kv, wide + own_prob * spread(nv_ref), 0.0)
    heads = wide[:, :HD]
    for k in range(1, KVH):
        heads = heads + wide[:, k * HD : (k + 1) * HD]
    rows = [
        jnp.concatenate([heads[n * QH + h : n * QH + h + 1] for h in range(QH)], axis=1)
        for n in range(len(places))
    ]
    attention = jnp.concatenate(rows, axis=0).astype(jnp.bfloat16)
    devices, _, part = out_ref.shape
    for d in range(devices):
        out_ref[d] = attention[:, d * part : (d + 1) * part]


PIECES = 4


def fetch_kernel(cuts, *refs):
    count = len(cuts)
    sources, targets, token, sems = refs[:count], refs[-count - 2 : -2], refs[-2], refs[-1]
    token[...] = jnp.zeros(token.shape, token.dtype)
    copies = []
    for source, target, cut in zip(sources, targets, cuts):
        if cut is None:
            copies.append(pltpu.make_async_copy(source, target, sems.at[len(copies)]))
        else:
            size = cut[1] // PIECES
            for at in range(0, cut[1], size):
                copies.append(
                    pltpu.make_async_copy(
                        source.at[pl.ds(cut[0] + at, size)],
                        target.at[pl.ds(at, size)],
                        sems.at[len(copies)],
                    )
                )
    for copy in copies:
        copy.start()
    for copy in copies:
        copy.wait()


def fetch(arrays, cuts, after, name):
    shapes = [a.shape if c is None else (c[1],) + a.shape[1:] for a, c in zip(arrays, cuts)]
    total = 2 * sum(math.prod(shape) for shape in shapes)
    copies = sum(1 if c is None else PIECES for c in cuts)
    return pl.pallas_call(
        lambda *refs: fetch_kernel(cuts, *refs),
        in_specs=[HBM] * len(arrays) + [ANY],
        out_specs=[VMEM] * (len(arrays) + 1),
        out_shape=[pltpu.VMEM(shape, a.dtype) for shape, a in zip(shapes, arrays)]
        + [jax.ShapeDtypeStruct((8, LANES), jnp.float32)],
        scratch_shapes=[pltpu.SemaphoreType.DMA((copies,))],
        compiler_params=params(8),
        cost_estimate=pl.CostEstimate(flops=0, bytes_accessed=total, transcendentals=0),
        name=name,
    )(*[far(a) for a in arrays], after)


def far(array):
    return pltpu.with_memory_space_constraint(array, pltpu.HBM)


def here(array):
    return pltpu.with_memory_space_constraint(array, pltpu.VMEM)


def rows_of(ref, order):
    blocks = [ref[d].astype(jnp.float32) for d in order]
    return jnp.concatenate(blocks, axis=0)


def send_blocks(refs, value, cut, rows):
    at = 0
    for ref in refs:
        for k in range(ref.shape[0]):
            ref[k, :, cut] = value[at : at + rows].astype(ref.dtype)
            at += rows


def project_kernel(order, x_ref, w_ref, *out_refs):
    rows, features = out_refs[0].shape[1:]
    me = lax.axis_index("dev")
    inputs = rows_of(x_ref, [me ^ k for k in order]).astype(jnp.bfloat16)
    for start in range(0, features, CHUNK):
        cut = slice(start, start + CHUNK)
        part = jnp.dot(inputs, w_ref[:, cut], preferred_element_type=jnp.float32)
        send_blocks(out_refs, part, cut, rows)


def total_of(refs):
    total = refs[0][...].astype(jnp.float32)
    for ref in refs[1:]:
        total = total + ref[...].astype(jnp.float32)
    return total


def fold_kernel(count, outs, *refs):
    total = total_of(refs[:count])
    at = 0
    for ref in refs[-outs:]:
        ref[...] = total[at : at + ref.shape[0]].astype(ref.dtype)
        at += ref.shape[0]


def fold(parts, outs, idle):
    blocks, rows, features = parts[0].shape
    shape = (blocks // outs, rows, features)
    return pl.pallas_call(
        lambda *refs: fold_kernel(len(parts), outs, *refs),
        in_specs=[VMEM] * len(parts) + [HBM] * len(idle),
        out_specs=[VMEM] * outs,
        out_shape=[jax.ShapeDtypeStruct(shape, jnp.float32)]
        + [jax.ShapeDtypeStruct(shape, jnp.bfloat16)] * (outs - 1),
        compiler_params=params(8),
        name="fold",
    )(*parts, *[far(a) for a in idle])


def norm_kernel(idx_ref, x_ref, gain_ref, router_ref, *refs):
    resid_ref, out_ref = refs[-2:]
    batches, sessions, features = x_ref.shape
    experts = router_ref.shape[0]
    rows = batches * sessions
    x_rows = jnp.concatenate([x_ref[m].astype(jnp.float32) for m in range(batches)], axis=0)
    resid = x_rows + total_of(refs[:-2])[0]
    resid_ref[...] = resid
    mean_square = jnp.mean(resid * resid, axis=1, keepdims=True)
    normed = (resid * lax.rsqrt(mean_square + 1e-05) * gain_ref[...].astype(jnp.float32).reshape(1, features)).astype(
        jnp.bfloat16
    )
    logits = lax.dot_general(
        normed, router_ref[...], (((1,), (1,)), ((), ())), preferred_element_type=jnp.float32
    )
    row = lax.broadcasted_iota(jnp.int32, (rows, experts), 0)
    column = lax.broadcasted_iota(jnp.int32, (rows, experts), 1)
    member = row < 0
    for m in range(batches):
        for s in range(sessions):
            for k in range(idx_ref.shape[2]):
                member = member | ((row == m * sessions + s) & (column == idx_ref[m, s, k]))
    peak = jnp.max(jnp.where(member, logits, -jnp.inf), axis=1, keepdims=True)
    mass = jnp.where(member, jnp.exp(logits - peak), 0.0)
    weights = mass / jnp.sum(mass, axis=1, keepdims=True)
    high = weights.astype(jnp.bfloat16).astype(jnp.float32)
    low = weights - high
    extra = jnp.concatenate(
        [high, low, jnp.zeros((rows, LANES - 2 * experts), jnp.float32)], axis=1
    ).astype(jnp.bfloat16)
    out_ref[0, :, :features] = normed
    out_ref[0, :, features:] = extra


def expert_kernel(expert_count, near_ref, far_ref, gate, up, down, *refs):
    out_refs, hidden = refs[:-1], refs[-1]
    rows, features = out_refs[0].shape[1:]
    units = hidden.shape[1]
    near, other = [[ref[d].astype(jnp.float32) for d in range(ref.shape[0])] for ref in (near_ref, far_ref)]
    blocks = near + other
    order, kept = scatter_order(len(blocks)), gather_order(len(blocks))
    whole = jnp.concatenate([blocks[kept.index(k)] for k in order], axis=0)
    inputs = whole[:, :features].astype(jnp.bfloat16)
    packed = whole[:, features:]
    expert = lax.div(lax.axis_index("dev"), len(blocks) // expert_count)
    lane = lax.broadcasted_iota(jnp.int32, packed.shape, 1)
    mine = (lane % expert_count == expert) & (lane < 2 * expert_count)
    weight = jnp.sum(jnp.where(mine, packed, 0.0), axis=1, keepdims=True)

    def product(weights, cut):
        return jnp.dot(inputs, weights[:, cut], preferred_element_type=jnp.float32)

    for start in range(0, units, CHUNK):
        cut = slice(start, start + CHUNK)
        hidden[:, cut] = (jax.nn.silu(product(gate, cut)) * product(up, cut)).astype(jnp.bfloat16)
    for start in range(0, features, CHUNK):
        cut = slice(start, start + CHUNK)
        part = jnp.dot(hidden[...], down[:, cut], preferred_element_type=jnp.float32)
        send_blocks(out_refs, part * weight, cut, rows)


def stages_of(devices):
    stages, bit = [], 2
    while bit < devices:
        if bit > 2 and 2 * bit < devices:
            stages.append((bit, 2 * bit, 3 * bit))
            bit *= 4
        else:
            stages.append((bit,))
            bit *= 2
    return stages


def gather_order(devices):
    order = [0]
    for masks in stages_of(devices):
        order = order + [mask ^ k for mask in masks for k in order]
    return order + [1 ^ k for k in order]


def scatter_order(devices):
    order = [0]
    for masks in reversed([(1,)] + stages_of(devices)):
        order = order + [mask ^ k for mask in masks for k in order]
    return order


def hop(blocks, mask):
    devices = lax.axis_size("dev")
    return lax.ppermute(blocks, "dev", [(i, i ^ mask) for i in range(devices)])


def gather(block, idle):
    for masks in stages_of(lax.axis_size("dev")):
        block = join([block] + [hop(block, mask) for mask in masks], idle)
    return block, hop(block, 1)


def join_kernel(count, *refs):
    size = refs[0].shape[0]
    for k in range(count):
        refs[-1][k * size : (k + 1) * size] = refs[k][...]


def join(parts, idle):
    shape = (len(parts) * parts[0].shape[0],) + parts[0].shape[1:]
    return pl.pallas_call(
        lambda *refs: join_kernel(len(parts), *refs),
        in_specs=[VMEM] * len(parts) + [HBM] * len(idle),
        out_specs=VMEM,
        out_shape=jax.ShapeDtypeStruct(shape, parts[0].dtype),
        compiler_params=params(8),
        name="join",
    )(*parts, *[far(a) for a in idle])


def scatter(keep, sends, idle):
    stages = [(1,)] + stages_of(lax.axis_size("dev"))
    for step, masks in enumerate(stages):
        parts = [keep] + [hop(block, mask) for block, mask in zip(sends, masks)]
        if step + 1 < len(stages):
            keep, *sends = fold(parts, len(stages[step + 1]) + 1, idle)
    return parts


def final_kernel(*refs):
    resid_ref, out_ref = refs[0], refs[-1]
    batches, sessions, _ = out_ref.shape
    mixed = resid_ref[...] + total_of(refs[1:-1])[0]
    for m in range(batches):
        out_ref[m] = mixed[m * sessions : (m + 1) * sessions].astype(jnp.bfloat16)


def exchange(blocks):
    return lax.all_to_all(blocks, "dev", split_axis=0, concat_axis=0, tiled=True)


def local(
    x_in,
    queries,
    cache_keys,
    cache_values,
    new_keys,
    new_values,
    lengths,
    w_out,
    norm_gain,
    w_router,
    experts_idx,
    w_gate,
    w_up,
    w_down,
):
    devices = lax.axis_size("dev")
    expert_count = w_router.shape[1]
    batches, sessions, features = x_in.shape
    rows = batches * sessions
    units = w_gate.shape[1]

    def blocks(width):
        return jax.ShapeDtypeStruct((devices, rows, width), jnp.bfloat16)

    operands = [lengths, queries, new_keys, cache_keys, new_values, cache_values]
    heads = pl.pallas_call(
        attend_kernel,
        in_specs=[HBM] * len(operands),
        out_specs=VMEM,
        out_shape=blocks(w_out.shape[0]),
        scratch_shapes=[pltpu.VMEM(a.shape, a.dtype) for a in operands]
        + [pltpu.SemaphoreType.DMA((len(operands),))],
        compiler_params=params(8),
        name="attend",
    )(*[far(a) for a in operands])
    head_blocks = exchange(heads)
    (out_here, _) = fetch([w_out], [None], heads, "fetch_out")
    halves = [jax.ShapeDtypeStruct((devices // 2, rows, features), t) for t in (jnp.float32, jnp.bfloat16)]
    keep, send = pl.pallas_call(
        lambda *refs: project_kernel(scatter_order(devices), *refs),
        in_specs=[VMEM] * 2,
        out_specs=[VMEM] * 2,
        out_shape=halves,
        compiler_params=params(8),
        name="project",
    )(head_blocks, here(out_here))
    attn_parts = scatter(keep, [send], [w_gate])
    resid, message = pl.pallas_call(
        norm_kernel,
        in_specs=[SMEM] + [VMEM] * (3 + len(attn_parts)),
        out_specs=(VMEM, VMEM),
        out_shape=(
            pltpu.VMEM((rows, features), jnp.float32),
            jax.ShapeDtypeStruct((1, rows, features + LANES), jnp.bfloat16),
        ),
        compiler_params=params(8),
        name="norm",
    )(experts_idx, here(x_in), norm_gain, jnp.transpose(w_router), *attn_parts)
    near, other = gather(message, [w_gate])
    keep, send = pl.pallas_call(
        lambda *refs: expert_kernel(expert_count, *refs),
        in_specs=[VMEM] * 5,
        out_specs=[VMEM] * 2,
        out_shape=halves,
        scratch_shapes=[
            pltpu.VMEM((devices * rows, units), jnp.bfloat16),
        ],
        compiler_params=params(8),
        name="experts",
    )(near, other, here(w_gate), here(w_up), here(w_down))
    parts = scatter(keep, [send], [])
    return pl.pallas_call(
        final_kernel,
        in_specs=[VMEM] * (1 + len(parts)),
        out_specs=VMEM,
        out_shape=jax.ShapeDtypeStruct(x_in.shape, jnp.bfloat16),
        compiler_params=params(8),
        name="final",
    )(resid, *parts)


def solution(mesh):
    return jax.shard_map(
        local,
        mesh=mesh,
        in_specs=(
            P(None, ("groups", "dev"), None),
            P(None, ("groups", "dev"), None),
            P(None, ("groups", "dev"), None, None),
            P(None, ("groups", "dev"), None, None),
            P(None, ("groups", "dev"), None),
            P(None, ("groups", "dev"), None),
            P(None, ("groups", "dev")),
            P("dev", None),
            P(),
            P(),
            P(None, ("groups", "dev"), None),
            P(None, "dev"),
            P(None, "dev"),
            P("dev", None),
        ),
        out_specs=P(None, ("groups", "dev"), None),
        check_vma=False,
    )
```

```python
import math

import jax
import jax.numpy as jnp
from jax import lax
from jax.experimental import pallas as pl
from jax.experimental.pallas import tpu as pltpu
from jax.sharding import PartitionSpec as P

QH = 24
KVH = 4
HD = 128
LANES = 128
CHUNK = 512
MIB = 1 << 20

VMEM = pl.BlockSpec(memory_space=pltpu.VMEM)
SMEM = pl.BlockSpec(memory_space=pltpu.SMEM)
HBM = pl.BlockSpec(memory_space=pltpu.HBM)
ANY = pl.BlockSpec(memory_space=pl.ANY)


def params(mib):
    return pltpu.CompilerParams(vmem_limit_bytes=mib * MIB)


def attend_kernel(*refs):
    count = (len(refs) - 2) // 2
    operands, out_ref, buffers, sems = refs[:count], refs[count], refs[count + 1 : -1], refs[-1]
    copies = [
        pltpu.make_async_copy(source, target, sems.at[i])
        for i, (source, target) in enumerate(zip(operands, buffers))
    ]
    for copy in copies:
        copy.start()
    for copy in copies:
        copy.wait()
    len_ref, q_ref, nk_ref, k_ref, nv_ref, v_ref = buffers
    batches, sessions = q_ref.shape[:2]
    places = [(m, s) for m in range(batches) for s in range(sessions)]
    cache_len = k_ref.shape[2]
    width = KVH * HD
    per_kv = QH // KVH
    scale = 1.0 / math.sqrt(HD)
    head = lax.broadcasted_iota(jnp.int32, (QH, width), 0) // per_kv
    lane = lax.broadcasted_iota(jnp.int32, (QH, width), 1) // HD
    own_kv = jnp.concatenate([head == lane] * len(places), axis=0)
    slot = lax.broadcasted_iota(jnp.int32, (QH, cache_len), 1)

    def each(piece):
        return jnp.concatenate([piece(m, s) for m, s in places], axis=0)

    def spread(ref):
        full = [ref[m].astype(jnp.float32) for m in range(batches)]
        return each(lambda m, s: jnp.broadcast_to(full[m][s : s + 1], (QH, width)))

    q_all = [q_ref[m].astype(jnp.float32) for m in range(batches)]
    q_heads = jnp.concatenate(
        [q_all[m][s : s + 1, h * HD : (h + 1) * HD] for m, s in places for h in range(QH)], axis=0
    )
    q_wide = jnp.where(own_kv, jnp.concatenate([q_heads] * KVH, axis=1), 0.0)
    q_narrow = q_wide.astype(jnp.bfloat16)
    scores = scale * jnp.concatenate(
        [
            lax.dot_general(
                q_narrow[n * QH : (n + 1) * QH],
                k_ref[m, s],
                (((1,), (1,)), ((), ())),
                preferred_element_type=jnp.float32,
            )
            for n, (m, s) in enumerate(places)
        ],
        axis=0,
    )
    own_score = jnp.sum(q_wide * spread(nk_ref), axis=1, keepdims=True) * scale
    live = each(lambda m, s: slot - len_ref[m, s : s + 1][:, None]) < 0
    peak = jnp.maximum(
        jnp.max(jnp.where(live, scores, -jnp.inf), axis=1, keepdims=True), own_score
    )
    mass = jnp.where(live, jnp.exp(scores - peak), 0.0)
    own_mass = jnp.exp(own_score - peak)
    total = jnp.sum(mass, axis=1, keepdims=True) + own_mass
    probs = (mass / total).astype(jnp.bfloat16)
    own_prob = (own_mass / total).astype(jnp.bfloat16).astype(jnp.float32)
    wide = jnp.concatenate(
        [
            jnp.dot(
                probs[n * QH : (n + 1) * QH], v_ref[m, s], preferred_element_type=jnp.float32
            )
            for n, (m, s) in enumerate(places)
        ],
        axis=0,
    )
    wide = jnp.where(own_kv, wide + own_prob * spread(nv_ref), 0.0)
    heads = wide[:, :HD]
    for k in range(1, KVH):
        heads = heads + wide[:, k * HD : (k + 1) * HD]
    rows = [
        jnp.concatenate([heads[n * QH + h : n * QH + h + 1] for h in range(QH)], axis=1)
        for n in range(len(places))
    ]
    attention = jnp.concatenate(rows, axis=0).astype(jnp.bfloat16)
    devices, _, part = out_ref.shape
    for d in range(devices):
        out_ref[d] = attention[:, d * part : (d + 1) * part]


PIECES = 4


def fetch_kernel(cuts, *refs):
    count = len(cuts)
    sources, targets, token, sems = refs[:count], refs[-count - 2 : -2], refs[-2], refs[-1]
    token[...] = jnp.zeros(token.shape, token.dtype)
    copies = []
    for source, target, cut in zip(sources, targets, cuts):
        if cut is None:
            copies.append(pltpu.make_async_copy(source, target, sems.at[len(copies)]))
        else:
            size = cut[1] // PIECES
            for at in range(0, cut[1], size):
                copies.append(
                    pltpu.make_async_copy(
                        source.at[pl.ds(cut[0] + at, size)],
                        target.at[pl.ds(at, size)],
                        sems.at[len(copies)],
                    )
                )
    for copy in copies:
        copy.start()
    for copy in copies:
        copy.wait()


def fetch(arrays, cuts, after, name):
    shapes = [a.shape if c is None else (c[1],) + a.shape[1:] for a, c in zip(arrays, cuts)]
    total = 2 * sum(math.prod(shape) for shape in shapes)
    copies = sum(1 if c is None else PIECES for c in cuts)
    return pl.pallas_call(
        lambda *refs: fetch_kernel(cuts, *refs),
        in_specs=[HBM] * len(arrays) + [ANY],
        out_specs=[VMEM] * (len(arrays) + 1),
        out_shape=[pltpu.VMEM(shape, a.dtype) for shape, a in zip(shapes, arrays)]
        + [jax.ShapeDtypeStruct((8, LANES), jnp.float32)],
        scratch_shapes=[pltpu.SemaphoreType.DMA((copies,))],
        compiler_params=params(8),
        cost_estimate=pl.CostEstimate(flops=0, bytes_accessed=total, transcendentals=0),
        name=name,
    )(*[far(a) for a in arrays], after)


def far(array):
    return pltpu.with_memory_space_constraint(array, pltpu.HBM)


def here(array):
    return pltpu.with_memory_space_constraint(array, pltpu.VMEM)


def rows_of(ref, order):
    blocks = [ref[d].astype(jnp.float32) for d in order]
    return jnp.concatenate(blocks, axis=0)


def send_blocks(refs, value, cut, rows):
    at = 0
    for ref in refs:
        for k in range(ref.shape[0]):
            ref[k, :, cut] = value[at : at + rows].astype(ref.dtype)
            at += rows


def project_kernel(order, x_ref, w_ref, *out_refs):
    rows, features = out_refs[0].shape[1:]
    me = lax.axis_index("dev")
    inputs = rows_of(x_ref, [me ^ k for k in order]).astype(jnp.bfloat16)
    for start in range(0, features, CHUNK):
        cut = slice(start, start + CHUNK)
        part = jnp.dot(inputs, w_ref[:, cut], preferred_element_type=jnp.float32)
        send_blocks(out_refs, part, cut, rows)


def total_of(refs):
    total = refs[0][...].astype(jnp.float32)
    for ref in refs[1:]:
        total = total + ref[...].astype(jnp.float32)
    return total


def fold_kernel(count, outs, *refs):
    total = total_of(refs[:count])
    at = 0
    for ref in refs[-outs:]:
        ref[...] = total[at : at + ref.shape[0]].astype(ref.dtype)
        at += ref.shape[0]


def fold(parts, outs, idle):
    blocks, rows, features = parts[0].shape
    shape = (blocks // outs, rows, features)
    return pl.pallas_call(
        lambda *refs: fold_kernel(len(parts), outs, *refs),
        in_specs=[VMEM] * len(parts) + [HBM] * len(idle),
        out_specs=[VMEM] * outs,
        out_shape=[jax.ShapeDtypeStruct(shape, jnp.float32)]
        + [jax.ShapeDtypeStruct(shape, jnp.bfloat16)] * (outs - 1),
        compiler_params=params(8),
        name="fold",
    )(*parts, *[far(a) for a in idle])


def share_kernel(count, idx_ref, x_ref, *refs):
    keep_ref, out_ref = refs[-2:]
    batches, sessions, features = x_ref.shape
    rows = batches * sessions
    total = total_of(refs[:count])
    x_rows = jnp.concatenate([x_ref[m].astype(jnp.float32) for m in range(batches)], axis=0)
    own = total[0] + x_rows
    row = lax.broadcasted_iota(jnp.int32, (rows, LANES), 0)
    column = lax.broadcasted_iota(jnp.int32, (rows, LANES), 1)
    member = jnp.zeros((rows, LANES), jnp.float32)
    for m in range(batches):
        for s in range(sessions):
            for k in range(idx_ref.shape[2]):
                hit = (row == m * sessions + s) & (column == idx_ref[m, s, k])
                member = jnp.where(hit, 1.0, member)
    keep_ref[0] = own
    keep_ref[1] = total[1]
    out_ref[0, :, :features] = own.astype(jnp.bfloat16)
    out_ref[1, :, :features] = total[1].astype(jnp.bfloat16)
    out_ref[0, :, features:] = member.astype(jnp.bfloat16)
    out_ref[1, :, features:] = jnp.zeros((rows, LANES), jnp.bfloat16)


def norm_kernel(gain_ref, router_ref, keep_ref, sent_ref, got_ref, *refs):
    resid_ref, out_ref = refs[-2:]
    rows, features = resid_ref.shape
    experts = router_ref.shape[0]
    got = got_ref[...].astype(jnp.float32)
    own = keep_ref[0] + got[1, :, :features]
    resid_ref[...] = own
    resid = jnp.concatenate([own, keep_ref[1] + got[0, :, :features]], axis=0)
    marks = jnp.concatenate([sent_ref[0, :, features:].astype(jnp.float32), got[0, :, features:]], axis=0)
    member = marks[:, :experts] > 0.5
    mean_square = jnp.mean(resid * resid, axis=1, keepdims=True)
    gain = gain_ref[...].astype(jnp.float32).reshape(1, features)
    normed = (resid * lax.rsqrt(mean_square + 1e-05) * gain).astype(jnp.bfloat16)
    logits = lax.dot_general(
        normed, router_ref[...], (((1,), (1,)), ((), ())), preferred_element_type=jnp.float32
    )
    peak = jnp.max(jnp.where(member, logits, -jnp.inf), axis=1, keepdims=True)
    mass = jnp.where(member, jnp.exp(logits - peak), 0.0)
    weights = mass / jnp.sum(mass, axis=1, keepdims=True)
    high = weights.astype(jnp.bfloat16).astype(jnp.float32)
    low = weights - high
    extra = jnp.concatenate(
        [high, low, jnp.zeros((2 * rows, LANES - 2 * experts), jnp.float32)], axis=1
    )
    for n in range(2):
        out_ref[n, :, :features] = normed[n * rows : (n + 1) * rows]
        out_ref[n, :, features:] = extra[n * rows : (n + 1) * rows].astype(jnp.bfloat16)


def expert_kernel(expert_count, near_ref, far_ref, gate, up, down, *refs):
    out_refs, hidden = refs[:-1], refs[-1]
    rows, features = out_refs[0].shape[1:]
    units = hidden.shape[1]
    near, other = [[ref[d].astype(jnp.float32) for d in range(ref.shape[0])] for ref in (near_ref, far_ref)]
    blocks = near + other
    order, kept = scatter_order(len(blocks)), gather_order(len(blocks))
    whole = jnp.concatenate([blocks[kept.index(k)] for k in order], axis=0)
    inputs = whole[:, :features].astype(jnp.bfloat16)
    packed = whole[:, features:]
    expert = lax.div(lax.axis_index("dev"), len(blocks) // expert_count)
    lane = lax.broadcasted_iota(jnp.int32, packed.shape, 1)
    mine = (lane % expert_count == expert) & (lane < 2 * expert_count)
    weight = jnp.sum(jnp.where(mine, packed, 0.0), axis=1, keepdims=True)

    def product(weights, cut):
        return jnp.dot(inputs, weights[:, cut], preferred_element_type=jnp.float32)

    for start in range(0, units, CHUNK):
        cut = slice(start, start + CHUNK)
        hidden[:, cut] = (jax.nn.silu(product(gate, cut)) * product(up, cut)).astype(jnp.bfloat16)
    for start in range(0, features, CHUNK):
        cut = slice(start, start + CHUNK)
        part = jnp.dot(hidden[...], down[:, cut], preferred_element_type=jnp.float32)
        send_blocks(out_refs, part * weight, cut, rows)


def stages_of(devices):
    stages, bit = [], 2
    while bit < devices:
        if bit > 2 and 2 * bit < devices:
            stages.append((bit, 2 * bit, 3 * bit))
            bit *= 4
        else:
            stages.append((bit,))
            bit *= 2
    return stages


def gather_order(devices):
    order = [0]
    for masks in stages_of(devices):
        order = order + [mask ^ k for mask in masks for k in order]
    return order + [1 ^ k for k in order]


def scatter_stages(devices):
    stages = stages_of(devices)
    return [(1,)] + stages[1:] + stages[:1]


def scatter_order(devices):
    order = [0]
    for masks in reversed(scatter_stages(devices)):
        order = order + [mask ^ k for mask in masks for k in order]
    return order


def hop(blocks, mask):
    devices = lax.axis_size("dev")
    return lax.ppermute(blocks, "dev", [(i, i ^ mask) for i in range(devices)])


def gather(block, idle):
    for masks in stages_of(lax.axis_size("dev"))[1:]:
        block = join([block] + [hop(block, mask) for mask in masks], idle)
    return block, hop(block, 1)


def join_kernel(count, *refs):
    size = refs[0].shape[0]
    for k in range(count):
        refs[-1][k * size : (k + 1) * size] = refs[k][...]


def join(parts, idle):
    shape = (len(parts) * parts[0].shape[0],) + parts[0].shape[1:]
    return pl.pallas_call(
        lambda *refs: join_kernel(len(parts), *refs),
        in_specs=[VMEM] * len(parts) + [HBM] * len(idle),
        out_specs=VMEM,
        out_shape=jax.ShapeDtypeStruct(shape, parts[0].dtype),
        compiler_params=params(8),
        name="join",
    )(*parts, *[far(a) for a in idle])


def scatter(keep, sends, idle, stages):
    for step, masks in enumerate(stages):
        parts = [keep] + [hop(block, mask) for block, mask in zip(sends, masks)]
        if step + 1 < len(stages):
            keep, *sends = fold(parts, len(stages[step + 1]) + 1, idle)
    return parts


def final_kernel(*refs):
    resid_ref, out_ref = refs[0], refs[-1]
    batches, sessions, _ = out_ref.shape
    mixed = resid_ref[...] + total_of(refs[1:-1])[0]
    for m in range(batches):
        out_ref[m] = mixed[m * sessions : (m + 1) * sessions].astype(jnp.bfloat16)


def exchange(blocks):
    return lax.all_to_all(blocks, "dev", split_axis=0, concat_axis=0, tiled=True)


def local(
    x_in,
    queries,
    cache_keys,
    cache_values,
    new_keys,
    new_values,
    lengths,
    w_out,
    norm_gain,
    w_router,
    experts_idx,
    w_gate,
    w_up,
    w_down,
):
    devices = lax.axis_size("dev")
    expert_count = w_router.shape[1]
    batches, sessions, features = x_in.shape
    rows = batches * sessions
    units = w_gate.shape[1]

    def blocks(width):
        return jax.ShapeDtypeStruct((devices, rows, width), jnp.bfloat16)

    operands = [lengths, queries, new_keys, cache_keys, new_values, cache_values]
    heads = pl.pallas_call(
        attend_kernel,
        in_specs=[HBM] * len(operands),
        out_specs=VMEM,
        out_shape=blocks(w_out.shape[0]),
        scratch_shapes=[pltpu.VMEM(a.shape, a.dtype) for a in operands]
        + [pltpu.SemaphoreType.DMA((len(operands),))],
        compiler_params=params(8),
        name="attend",
    )(*[far(a) for a in operands])
    head_blocks = exchange(heads)
    (out_here, _) = fetch([w_out], [None], heads, "fetch_out")
    halves = [jax.ShapeDtypeStruct((devices // 2, rows, features), t) for t in (jnp.float32, jnp.bfloat16)]
    keep, send = pl.pallas_call(
        lambda *refs: project_kernel(scatter_order(devices), *refs),
        in_specs=[VMEM] * 2,
        out_specs=[VMEM] * 2,
        out_shape=halves,
        compiler_params=params(8),
        name="project",
    )(head_blocks, here(out_here))
    stages = scatter_stages(devices)
    attn_parts = scatter(keep, [send], [w_gate], stages[:-1])
    wide = jax.ShapeDtypeStruct((2, rows, features + LANES), jnp.bfloat16)
    keep, send = pl.pallas_call(
        lambda *refs: share_kernel(len(attn_parts), *refs),
        in_specs=[SMEM] + [VMEM] * (1 + len(attn_parts)) + [HBM],
        out_specs=(VMEM, VMEM),
        out_shape=(jax.ShapeDtypeStruct((2, rows, features), jnp.float32), wide),
        compiler_params=params(8),
        name="share",
    )(experts_idx, here(x_in), *attn_parts, far(w_gate))
    resid, message = pl.pallas_call(
        norm_kernel,
        in_specs=[VMEM] * 5 + [HBM],
        out_specs=(VMEM, VMEM),
        out_shape=(pltpu.VMEM((rows, features), jnp.float32), wide),
        compiler_params=params(8),
        name="norm",
    )(norm_gain, jnp.transpose(w_router), keep, send, hop(send, stages[-1][0]), far(w_gate))
    near, other = gather(message, [w_gate])
    keep, send = pl.pallas_call(
        lambda *refs: expert_kernel(expert_count, *refs),
        in_specs=[VMEM] * 5,
        out_specs=[VMEM] * 2,
        out_shape=halves,
        scratch_shapes=[
            pltpu.VMEM((devices * rows, units), jnp.bfloat16),
        ],
        compiler_params=params(8),
        name="experts",
    )(near, other, here(w_gate), here(w_up), here(w_down))
    parts = scatter(keep, [send], [], stages)
    return pl.pallas_call(
        final_kernel,
        in_specs=[VMEM] * (1 + len(parts)),
        out_specs=VMEM,
        out_shape=jax.ShapeDtypeStruct(x_in.shape, jnp.bfloat16),
        compiler_params=params(8),
        name="final",
    )(resid, *parts)


def solution(mesh):
    return jax.shard_map(
        local,
        mesh=mesh,
        in_specs=(
            P(None, ("groups", "dev"), None),
            P(None, ("groups", "dev"), None),
            P(None, ("groups", "dev"), None, None),
            P(None, ("groups", "dev"), None, None),
            P(None, ("groups", "dev"), None),
            P(None, ("groups", "dev"), None),
            P(None, ("groups", "dev")),
            P("dev", None),
            P(),
            P(),
            P(None, ("groups", "dev"), None),
            P(None, "dev"),
            P(None, "dev"),
            P("dev", None),
        ),
        out_specs=P(None, ("groups", "dev"), None),
        check_vma=False,
    )
```

```python
import math

import jax
import jax.numpy as jnp
from jax import lax
from jax.experimental import pallas as pl
from jax.experimental.pallas import tpu as pltpu
from jax.sharding import PartitionSpec as P

QH = 24
KVH = 4
HD = 128
LANES = 128
CHUNK = 512
MIB = 1 << 20

VMEM = pl.BlockSpec(memory_space=pltpu.VMEM)
SMEM = pl.BlockSpec(memory_space=pltpu.SMEM)
HBM = pl.BlockSpec(memory_space=pltpu.HBM)
ANY = pl.BlockSpec(memory_space=pl.ANY)


def params(mib):
    return pltpu.CompilerParams(vmem_limit_bytes=mib * MIB)


def attend_kernel(*refs):
    count = (len(refs) - 2) // 2
    operands, out_ref, buffers, sems = refs[:count], refs[count], refs[count + 1 : -1], refs[-1]
    copies = [
        pltpu.make_async_copy(source, target, sems.at[i])
        for i, (source, target) in enumerate(zip(operands, buffers))
    ]
    for copy in copies:
        copy.start()
    for copy in copies:
        copy.wait()
    len_ref, q_ref, nk_ref, k_ref, nv_ref, v_ref = buffers
    batches, sessions = q_ref.shape[:2]
    places = [(m, s) for m in range(batches) for s in range(sessions)]
    cache_len = k_ref.shape[2]
    width = KVH * HD
    per_kv = QH // KVH
    scale = 1.0 / math.sqrt(HD)
    head = lax.broadcasted_iota(jnp.int32, (QH, width), 0) // per_kv
    lane = lax.broadcasted_iota(jnp.int32, (QH, width), 1) // HD
    own_kv = jnp.concatenate([head == lane] * len(places), axis=0)
    slot = lax.broadcasted_iota(jnp.int32, (QH, cache_len), 1)

    def each(piece):
        return jnp.concatenate([piece(m, s) for m, s in places], axis=0)

    def spread(ref):
        full = [ref[m].astype(jnp.float32) for m in range(batches)]
        return each(lambda m, s: jnp.broadcast_to(full[m][s : s + 1], (QH, width)))

    q_all = [q_ref[m].astype(jnp.float32) for m in range(batches)]
    q_heads = jnp.concatenate(
        [q_all[m][s : s + 1, h * HD : (h + 1) * HD] for m, s in places for h in range(QH)], axis=0
    )
    q_wide = jnp.where(own_kv, jnp.concatenate([q_heads] * KVH, axis=1), 0.0)
    q_narrow = q_wide.astype(jnp.bfloat16)
    scores = scale * jnp.concatenate(
        [
            lax.dot_general(
                q_narrow[n * QH : (n + 1) * QH],
                k_ref[m, s],
                (((1,), (1,)), ((), ())),
                preferred_element_type=jnp.float32,
            )
            for n, (m, s) in enumerate(places)
        ],
        axis=0,
    )
    own_score = jnp.sum(q_wide * spread(nk_ref), axis=1, keepdims=True) * scale
    live = each(lambda m, s: slot - len_ref[m, s : s + 1][:, None]) < 0
    peak = jnp.maximum(
        jnp.max(jnp.where(live, scores, -jnp.inf), axis=1, keepdims=True), own_score
    )
    mass = jnp.where(live, jnp.exp(scores - peak), 0.0)
    own_mass = jnp.exp(own_score - peak)
    total = jnp.sum(mass, axis=1, keepdims=True) + own_mass
    probs = (mass / total).astype(jnp.bfloat16)
    own_prob = (own_mass / total).astype(jnp.bfloat16).astype(jnp.float32)
    wide = jnp.concatenate(
        [
            jnp.dot(
                probs[n * QH : (n + 1) * QH], v_ref[m, s], preferred_element_type=jnp.float32
            )
            for n, (m, s) in enumerate(places)
        ],
        axis=0,
    )
    wide = jnp.where(own_kv, wide + own_prob * spread(nv_ref), 0.0)
    heads = wide[:, :HD]
    for k in range(1, KVH):
        heads = heads + wide[:, k * HD : (k + 1) * HD]
    rows = [
        jnp.concatenate([heads[n * QH + h : n * QH + h + 1] for h in range(QH)], axis=1)
        for n in range(len(places))
    ]
    attention = jnp.concatenate(rows, axis=0).astype(jnp.bfloat16)
    devices, _, part = out_ref.shape
    for d in range(devices):
        out_ref[d] = attention[:, d * part : (d + 1) * part]


PIECES = 4


def fetch_kernel(cuts, *refs):
    count = len(cuts)
    sources, targets, token, sems = refs[:count], refs[-count - 2 : -2], refs[-2], refs[-1]
    token[...] = jnp.zeros(token.shape, token.dtype)
    copies = []
    for source, target, cut in zip(sources, targets, cuts):
        if cut is None:
            copies.append(pltpu.make_async_copy(source, target, sems.at[len(copies)]))
        else:
            size = cut[1] // PIECES
            for at in range(0, cut[1], size):
                copies.append(
                    pltpu.make_async_copy(
                        source.at[pl.ds(cut[0] + at, size)],
                        target.at[pl.ds(at, size)],
                        sems.at[len(copies)],
                    )
                )
    for copy in copies:
        copy.start()
    for copy in copies:
        copy.wait()


def fetch(arrays, cuts, after, name):
    shapes = [a.shape if c is None else (c[1],) + a.shape[1:] for a, c in zip(arrays, cuts)]
    total = 2 * sum(math.prod(shape) for shape in shapes)
    copies = sum(1 if c is None else PIECES for c in cuts)
    return pl.pallas_call(
        lambda *refs: fetch_kernel(cuts, *refs),
        in_specs=[HBM] * len(arrays) + [ANY],
        out_specs=[VMEM] * (len(arrays) + 1),
        out_shape=[pltpu.VMEM(shape, a.dtype) for shape, a in zip(shapes, arrays)]
        + [jax.ShapeDtypeStruct((8, LANES), jnp.float32)],
        scratch_shapes=[pltpu.SemaphoreType.DMA((copies,))],
        compiler_params=params(8),
        cost_estimate=pl.CostEstimate(flops=0, bytes_accessed=total, transcendentals=0),
        name=name,
    )(*[far(a) for a in arrays], after)


def far(array):
    return pltpu.with_memory_space_constraint(array, pltpu.HBM)


def here(array):
    return pltpu.with_memory_space_constraint(array, pltpu.VMEM)


def rows_of(ref, order):
    blocks = [ref[d].astype(jnp.float32) for d in order]
    return jnp.concatenate(blocks, axis=0)


def send_blocks(refs, value, cut, rows):
    at = 0
    for ref in refs:
        for k in range(ref.shape[0]):
            ref[k, :, cut] = value[at : at + rows].astype(ref.dtype)
            at += rows


def project_kernel(order, x_ref, w_ref, other_ref, _, *out_refs):
    rows, features = out_refs[0].shape[1:]
    half = w_ref.shape[0]
    me = lax.axis_index("dev")
    inputs = rows_of(x_ref, [lax.div(me ^ k, 2) for k in order])
    even = lax.rem(me, 2) == 0
    mine = jnp.where(even, inputs[:, :half], inputs[:, half:]).astype(jnp.bfloat16)
    others = jnp.where(even, inputs[:, half:], inputs[:, :half]).astype(jnp.bfloat16)
    for start in range(0, features, CHUNK):
        cut = slice(start, start + CHUNK)
        part = jnp.dot(mine, w_ref[:, cut], preferred_element_type=jnp.float32)
        part = part + jnp.dot(others, other_ref[:, cut], preferred_element_type=jnp.float32)
        send_blocks(out_refs, part, cut, rows)


def total_of(refs):
    total = refs[0][...].astype(jnp.float32)
    for ref in refs[1:]:
        total = total + ref[...].astype(jnp.float32)
    return total


def fold_kernel(count, outs, *refs):
    total = total_of(refs[:count])
    at = 0
    for ref in refs[-outs:]:
        ref[...] = total[at : at + ref.shape[0]].astype(ref.dtype)
        at += ref.shape[0]


def fold(parts, outs, idle):
    blocks, rows, features = parts[0].shape
    shape = (blocks // outs, rows, features)
    return pl.pallas_call(
        lambda *refs: fold_kernel(len(parts), outs, *refs),
        in_specs=[VMEM] * len(parts) + [HBM] * len(idle),
        out_specs=[VMEM] * outs,
        out_shape=[jax.ShapeDtypeStruct(shape, jnp.float32)]
        + [jax.ShapeDtypeStruct(shape, jnp.bfloat16)] * (outs - 1),
        compiler_params=params(8),
        name="fold",
    )(*parts, *[far(a) for a in idle])


def share_kernel(count, idx_ref, x_ref, *refs):
    keep_ref, out_ref = refs[-2:]
    batches, sessions, features = x_ref.shape
    rows = batches * sessions
    total = total_of(refs[:count])
    x_rows = jnp.concatenate([x_ref[m].astype(jnp.float32) for m in range(batches)], axis=0)
    own = total[0] + x_rows
    row = lax.broadcasted_iota(jnp.int32, (rows, LANES), 0)
    column = lax.broadcasted_iota(jnp.int32, (rows, LANES), 1)
    member = jnp.zeros((rows, LANES), jnp.float32)
    for m in range(batches):
        for s in range(sessions):
            for k in range(idx_ref.shape[2]):
                hit = (row == m * sessions + s) & (column == idx_ref[m, s, k])
                member = jnp.where(hit, 1.0, member)
    keep_ref[0] = own
    keep_ref[1] = total[1]
    out_ref[0, :, :features] = own.astype(jnp.bfloat16)
    out_ref[1, :, :features] = total[1].astype(jnp.bfloat16)
    out_ref[0, :, features:] = member.astype(jnp.bfloat16)
    out_ref[1, :, features:] = jnp.zeros((rows, LANES), jnp.bfloat16)


def norm_kernel(gain_ref, router_ref, keep_ref, sent_ref, got_ref, *refs):
    resid_ref, out_ref = refs[-2:]
    rows, features = resid_ref.shape
    experts = router_ref.shape[0]
    got = got_ref[...].astype(jnp.float32)
    own = keep_ref[0] + got[1, :, :features]
    resid_ref[...] = own
    resid = jnp.concatenate([own, keep_ref[1] + got[0, :, :features]], axis=0)
    marks = jnp.concatenate([sent_ref[0, :, features:].astype(jnp.float32), got[0, :, features:]], axis=0)
    member = marks[:, :experts] > 0.5
    mean_square = jnp.mean(resid * resid, axis=1, keepdims=True)
    gain = gain_ref[...].astype(jnp.float32).reshape(1, features)
    normed = (resid * lax.rsqrt(mean_square + 1e-05) * gain).astype(jnp.bfloat16)
    logits = lax.dot_general(
        normed, router_ref[...], (((1,), (1,)), ((), ())), preferred_element_type=jnp.float32
    )
    peak = jnp.max(jnp.where(member, logits, -jnp.inf), axis=1, keepdims=True)
    mass = jnp.where(member, jnp.exp(logits - peak), 0.0)
    weights = mass / jnp.sum(mass, axis=1, keepdims=True)
    high = weights.astype(jnp.bfloat16).astype(jnp.float32)
    low = weights - high
    extra = jnp.concatenate(
        [high, low, jnp.zeros((2 * rows, LANES - 2 * experts), jnp.float32)], axis=1
    )
    for n in range(2):
        out_ref[n, :, :features] = normed[n * rows : (n + 1) * rows]
        out_ref[n, :, features:] = extra[n * rows : (n + 1) * rows].astype(jnp.bfloat16)


def expert_kernel(expert_count, near_ref, far_ref, gate, up, down, *refs):
    out_refs, hidden = refs[:-1], refs[-1]
    rows, features = out_refs[0].shape[1:]
    units = hidden.shape[1]
    near, other = [[ref[d].astype(jnp.float32) for d in range(ref.shape[0])] for ref in (near_ref, far_ref)]
    blocks = near + other
    order, kept = scatter_order(len(blocks)), gather_order(len(blocks))
    whole = jnp.concatenate([blocks[kept.index(k)] for k in order], axis=0)
    inputs = whole[:, :features].astype(jnp.bfloat16)
    packed = whole[:, features:]
    expert = lax.div(lax.axis_index("dev"), len(blocks) // expert_count)
    lane = lax.broadcasted_iota(jnp.int32, packed.shape, 1)
    mine = (lane % expert_count == expert) & (lane < 2 * expert_count)
    weight = jnp.sum(jnp.where(mine, packed, 0.0), axis=1, keepdims=True)

    def product(weights, cut):
        return jnp.dot(inputs, weights[:, cut], preferred_element_type=jnp.float32)

    for start in range(0, units, CHUNK):
        cut = slice(start, start + CHUNK)
        hidden[:, cut] = (jax.nn.silu(product(gate, cut)) * product(up, cut)).astype(jnp.bfloat16)
    for start in range(0, features, CHUNK):
        cut = slice(start, start + CHUNK)
        part = jnp.dot(hidden[...], down[:, cut], preferred_element_type=jnp.float32)
        send_blocks(out_refs, part * weight, cut, rows)


def stages_of(devices):
    stages, bit = [], 2
    while bit < devices:
        if bit > 2 and 2 * bit < devices:
            stages.append((bit, 2 * bit, 3 * bit))
            bit *= 4
        else:
            stages.append((bit,))
            bit *= 2
    return stages


def gather_order(devices):
    order = [0]
    for masks in stages_of(devices):
        order = order + [mask ^ k for mask in masks for k in order]
    return order + [1 ^ k for k in order]


def scatter_stages(devices):
    stages = stages_of(devices)
    return [(1,)] + stages[1:] + stages[:1]


def scatter_order(devices):
    return nested(scatter_stages(devices))


def nested(stages):
    order = [0]
    for masks in reversed(stages):
        order = order + [mask ^ k for mask in masks for k in order]
    return order


def hop(blocks, mask):
    devices = lax.axis_size("dev")
    return lax.ppermute(blocks, "dev", [(i, i ^ mask) for i in range(devices)])


def gather(block, idle):
    for masks in stages_of(lax.axis_size("dev"))[1:]:
        block = join([block] + [hop(block, mask) for mask in masks], idle)
    return block, hop(block, 1)


def join_kernel(count, *refs):
    size = refs[0].shape[0]
    for k in range(count):
        refs[-1][k * size : (k + 1) * size] = refs[k][...]


def join(parts, idle):
    shape = (len(parts) * parts[0].shape[0],) + parts[0].shape[1:]
    return pl.pallas_call(
        lambda *refs: join_kernel(len(parts), *refs),
        in_specs=[VMEM] * len(parts) + [HBM] * len(idle),
        out_specs=VMEM,
        out_shape=jax.ShapeDtypeStruct(shape, parts[0].dtype),
        compiler_params=params(8),
        name="join",
    )(*parts, *[far(a) for a in idle])


def scatter(keep, sends, idle, stages):
    for step, masks in enumerate(stages):
        parts = [keep] + [hop(block, mask) for block, mask in zip(sends, masks)]
        if step + 1 < len(stages):
            keep, *sends = fold(parts, len(stages[step + 1]) + 1, idle)
    return parts


def final_kernel(*refs):
    resid_ref, out_ref = refs[0], refs[-1]
    batches, sessions, _ = out_ref.shape
    mixed = resid_ref[...] + total_of(refs[1:-1])[0]
    for m in range(batches):
        out_ref[m] = mixed[m * sessions : (m + 1) * sessions].astype(jnp.bfloat16)


def exchange(blocks):
    devices = lax.axis_size("dev")
    groups = [list(range(core, devices, 2)) for core in range(2)]
    return lax.all_to_all(
        blocks, "dev", split_axis=0, concat_axis=0, axis_index_groups=groups, tiled=True
    )


def local(
    x_in,
    queries,
    cache_keys,
    cache_values,
    new_keys,
    new_values,
    lengths,
    w_out,
    norm_gain,
    w_router,
    experts_idx,
    w_gate,
    w_up,
    w_down,
):
    devices = lax.axis_size("dev")
    expert_count = w_router.shape[1]
    batches, sessions, features = x_in.shape
    rows = batches * sessions
    units = w_gate.shape[1]

    operands = [lengths, queries, new_keys, cache_keys, new_values, cache_values]
    heads = pl.pallas_call(
        attend_kernel,
        in_specs=[HBM] * len(operands),
        out_specs=VMEM,
        out_shape=jax.ShapeDtypeStruct((devices // 2, rows, 2 * w_out.shape[0]), jnp.bfloat16),
        scratch_shapes=[pltpu.VMEM(a.shape, a.dtype) for a in operands]
        + [pltpu.SemaphoreType.DMA((len(operands),))],
        compiler_params=params(8),
        name="attend",
    )(*[far(a) for a in operands])
    head_blocks = exchange(heads)
    (out_here, _) = fetch([w_out], [None], heads, "fetch_out")
    out_other = hop(w_out, 1)
    halves = [jax.ShapeDtypeStruct((devices // 2, rows, features), t) for t in (jnp.float32, jnp.bfloat16)]
    stages = scatter_stages(devices)
    first = (devices // 2) // (len(stages[1]) + 1)
    keep, *sends = pl.pallas_call(
        lambda *refs: project_kernel(nested(stages[1:]), *refs),
        in_specs=[VMEM] * 3 + [HBM],
        out_specs=[VMEM] * (len(stages[1]) + 1),
        out_shape=[jax.ShapeDtypeStruct((first, rows, features), jnp.float32)]
        + [jax.ShapeDtypeStruct((first, rows, features), jnp.bfloat16)] * len(stages[1]),
        compiler_params=params(8),
        name="project",
    )(head_blocks, here(out_here), here(out_other), far(w_gate))
    attn_parts = scatter(keep, sends, [w_gate], stages[1:-1])
    wide = jax.ShapeDtypeStruct((2, rows, features + LANES), jnp.bfloat16)
    keep, send = pl.pallas_call(
        lambda *refs: share_kernel(len(attn_parts), *refs),
        in_specs=[SMEM] + [VMEM] * (1 + len(attn_parts)) + [HBM],
        out_specs=(VMEM, VMEM),
        out_shape=(jax.ShapeDtypeStruct((2, rows, features), jnp.float32), wide),
        compiler_params=params(8),
        name="share",
    )(experts_idx, here(x_in), *attn_parts, far(w_gate))
    resid, message = pl.pallas_call(
        norm_kernel,
        in_specs=[VMEM] * 5 + [HBM],
        out_specs=(VMEM, VMEM),
        out_shape=(pltpu.VMEM((rows, features), jnp.float32), wide),
        compiler_params=params(8),
        name="norm",
    )(norm_gain, jnp.transpose(w_router), keep, send, hop(send, stages[-1][0]), far(w_gate))
    near, other = gather(message, [w_gate])
    keep, send = pl.pallas_call(
        lambda *refs: expert_kernel(expert_count, *refs),
        in_specs=[VMEM] * 5,
        out_specs=[VMEM] * 2,
        out_shape=halves,
        scratch_shapes=[
            pltpu.VMEM((devices * rows, units), jnp.bfloat16),
        ],
        compiler_params=params(8),
        name="experts",
    )(near, other, here(w_gate), here(w_up), here(w_down))
    parts = scatter(keep, [send], [], stages)
    return pl.pallas_call(
        final_kernel,
        in_specs=[VMEM] * (1 + len(parts)),
        out_specs=VMEM,
        out_shape=jax.ShapeDtypeStruct(x_in.shape, jnp.bfloat16),
        compiler_params=params(8),
        name="final",
    )(resid, *parts)


def solution(mesh):
    return jax.shard_map(
        local,
        mesh=mesh,
        in_specs=(
            P(None, ("groups", "dev"), None),
            P(None, ("groups", "dev"), None),
            P(None, ("groups", "dev"), None, None),
            P(None, ("groups", "dev"), None, None),
            P(None, ("groups", "dev"), None),
            P(None, ("groups", "dev"), None),
            P(None, ("groups", "dev")),
            P("dev", None),
            P(),
            P(),
            P(None, ("groups", "dev"), None),
            P(None, "dev"),
            P(None, "dev"),
            P("dev", None),
        ),
        out_specs=P(None, ("groups", "dev"), None),
        check_vma=False,
    )
```

```python
import math

import jax
import jax.numpy as jnp
from jax import lax
from jax.experimental import pallas as pl
from jax.experimental.pallas import tpu as pltpu
from jax.sharding import PartitionSpec as P

QH = 24
KVH = 4
HD = 128
LANES = 128
CHUNK = 512
MIB = 1 << 20

VMEM = pl.BlockSpec(memory_space=pltpu.VMEM)
SMEM = pl.BlockSpec(memory_space=pltpu.SMEM)
HBM = pl.BlockSpec(memory_space=pltpu.HBM)
ANY = pl.BlockSpec(memory_space=pl.ANY)


def params(mib):
    return pltpu.CompilerParams(vmem_limit_bytes=mib * MIB)


def attend_kernel(*refs):
    count = (len(refs) - 2) // 2
    operands, out_ref, w_ref = refs[:count], refs[count], refs[count + 1]
    buffers, sems = refs[count + 2 : -1] + (w_ref,), refs[-1]
    copies = [
        pltpu.make_async_copy(source, target, sems.at[i])
        for i, (source, target) in enumerate(zip(operands, buffers))
    ]
    for copy in copies:
        copy.start()
    q_ref, k_ref, nk_ref, len_ref, v_ref, nv_ref, _ = buffers
    for copy in copies[:4]:
        copy.wait()
    batches, sessions = q_ref.shape[:2]
    places = [(m, s) for m in range(batches) for s in range(sessions)]
    cache_len = k_ref.shape[2]
    width = KVH * HD
    per_kv = QH // KVH
    scale = 1.0 / math.sqrt(HD)
    head = lax.broadcasted_iota(jnp.int32, (QH, width), 0) // per_kv
    lane = lax.broadcasted_iota(jnp.int32, (QH, width), 1) // HD
    own_kv = jnp.concatenate([head == lane] * len(places), axis=0)
    slot = lax.broadcasted_iota(jnp.int32, (QH, cache_len), 1)

    def each(piece):
        return jnp.concatenate([piece(m, s) for m, s in places], axis=0)

    def spread(ref):
        full = [ref[m].astype(jnp.float32) for m in range(batches)]
        return each(lambda m, s: jnp.broadcast_to(full[m][s : s + 1], (QH, width)))

    q_all = [q_ref[m].astype(jnp.float32) for m in range(batches)]
    q_heads = jnp.concatenate(
        [q_all[m][s : s + 1, h * HD : (h + 1) * HD] for m, s in places for h in range(QH)], axis=0
    )
    q_wide = jnp.where(own_kv, jnp.concatenate([q_heads] * KVH, axis=1), 0.0)
    q_narrow = q_wide.astype(jnp.bfloat16)
    scores = scale * jnp.concatenate(
        [
            lax.dot_general(
                q_narrow[n * QH : (n + 1) * QH],
                k_ref[m, s],
                (((1,), (1,)), ((), ())),
                preferred_element_type=jnp.float32,
            )
            for n, (m, s) in enumerate(places)
        ],
        axis=0,
    )
    own_score = jnp.sum(q_wide * spread(nk_ref), axis=1, keepdims=True) * scale
    live = each(lambda m, s: slot - len_ref[m, s : s + 1][:, None]) < 0
    peak = jnp.maximum(
        jnp.max(jnp.where(live, scores, -jnp.inf), axis=1, keepdims=True), own_score
    )
    mass = jnp.where(live, jnp.exp(scores - peak), 0.0)
    own_mass = jnp.exp(own_score - peak)
    total = jnp.sum(mass, axis=1, keepdims=True) + own_mass
    probs = (mass / total).astype(jnp.bfloat16)
    own_prob = (own_mass / total).astype(jnp.bfloat16).astype(jnp.float32)
    for copy in copies[4:6]:
        copy.wait()
    wide = jnp.concatenate(
        [
            jnp.dot(
                probs[n * QH : (n + 1) * QH], v_ref[m, s], preferred_element_type=jnp.float32
            )
            for n, (m, s) in enumerate(places)
        ],
        axis=0,
    )
    wide = jnp.where(own_kv, wide + own_prob * spread(nv_ref), 0.0)
    heads = wide[:, :HD]
    for k in range(1, KVH):
        heads = heads + wide[:, k * HD : (k + 1) * HD]
    rows = [
        jnp.concatenate([heads[n * QH + h : n * QH + h + 1] for h in range(QH)], axis=1)
        for n in range(len(places))
    ]
    attention = jnp.concatenate(rows, axis=0).astype(jnp.bfloat16)
    devices, _, part = out_ref.shape
    for d in range(devices):
        out_ref[d] = attention[:, d * part : (d + 1) * part]
    copies[6].wait()


def far(array):
    return pltpu.with_memory_space_constraint(array, pltpu.HBM)


def here(array):
    return pltpu.with_memory_space_constraint(array, pltpu.VMEM)


def rows_of(ref, order):
    blocks = [ref[d].astype(jnp.float32) for d in order]
    return jnp.concatenate(blocks, axis=0)


def send_blocks(refs, value, cut, rows):
    at = 0
    for ref in refs:
        for k in range(ref.shape[0]):
            ref[k, :, cut] = value[at : at + rows].astype(ref.dtype)
            at += rows


def project_kernel(order, x_ref, w_ref, other_ref, _, *out_refs):
    rows, features = out_refs[0].shape[1:]
    half = w_ref.shape[0]
    me = lax.axis_index("dev")
    inputs = rows_of(x_ref, [lax.div(me ^ k, 2) for k in order])
    even = lax.rem(me, 2) == 0
    mine = jnp.where(even, inputs[:, :half], inputs[:, half:]).astype(jnp.bfloat16)
    others = jnp.where(even, inputs[:, half:], inputs[:, :half]).astype(jnp.bfloat16)
    for start in range(0, features, CHUNK):
        cut = slice(start, start + CHUNK)
        part = jnp.dot(mine, w_ref[:, cut], preferred_element_type=jnp.float32)
        part = part + jnp.dot(others, other_ref[:, cut], preferred_element_type=jnp.float32)
        send_blocks(out_refs, part, cut, rows)


def total_of(refs):
    total = refs[0][...].astype(jnp.float32)
    for ref in refs[1:]:
        total = total + ref[...].astype(jnp.float32)
    return total


def fold_kernel(count, outs, *refs):
    total = total_of(refs[:count])
    at = 0
    for ref in refs[-outs:]:
        ref[...] = total[at : at + ref.shape[0]].astype(ref.dtype)
        at += ref.shape[0]


def fold(parts, outs, idle):
    blocks, rows, features = parts[0].shape
    shape = (blocks // outs, rows, features)
    return pl.pallas_call(
        lambda *refs: fold_kernel(len(parts), outs, *refs),
        in_specs=[VMEM] * len(parts) + [HBM] * len(idle),
        out_specs=[VMEM] * outs,
        out_shape=[jax.ShapeDtypeStruct(shape, jnp.float32)]
        + [jax.ShapeDtypeStruct(shape, jnp.bfloat16)] * (outs - 1),
        compiler_params=params(8),
        name="fold",
    )(*parts, *[far(a) for a in idle])


def share_kernel(count, idx_ref, x_ref, *refs):
    keep_ref, out_ref = refs[-2:]
    batches, sessions, features = x_ref.shape
    rows = batches * sessions
    total = total_of(refs[:count])
    x_rows = jnp.concatenate([x_ref[m].astype(jnp.float32) for m in range(batches)], axis=0)
    own = total[0] + x_rows
    row = lax.broadcasted_iota(jnp.int32, (rows, LANES), 0)
    column = lax.broadcasted_iota(jnp.int32, (rows, LANES), 1)
    member = jnp.zeros((rows, LANES), jnp.float32)
    for m in range(batches):
        for s in range(sessions):
            for k in range(idx_ref.shape[2]):
                hit = (row == m * sessions + s) & (column == idx_ref[m, s, k])
                member = jnp.where(hit, 1.0, member)
    keep_ref[0] = own
    keep_ref[1] = total[1]
    out_ref[0, :, :features] = own.astype(jnp.bfloat16)
    out_ref[1, :, :features] = total[1].astype(jnp.bfloat16)
    out_ref[0, :, features:] = member.astype(jnp.bfloat16)
    out_ref[1, :, features:] = jnp.zeros((rows, LANES), jnp.bfloat16)


def norm_kernel(gain_ref, router_ref, keep_ref, sent_ref, got_ref, *refs):
    resid_ref, out_ref = refs[-2:]
    rows, features = resid_ref.shape
    experts = router_ref.shape[0]
    got = got_ref[...].astype(jnp.float32)
    own = keep_ref[0] + got[1, :, :features]
    resid_ref[...] = own
    resid = jnp.concatenate([own, keep_ref[1] + got[0, :, :features]], axis=0)
    marks = jnp.concatenate([sent_ref[0, :, features:].astype(jnp.float32), got[0, :, features:]], axis=0)
    member = marks[:, :experts] > 0.5
    mean_square = jnp.mean(resid * resid, axis=1, keepdims=True)
    gain = gain_ref[...].astype(jnp.float32).reshape(1, features)
    normed = (resid * lax.rsqrt(mean_square + 1e-05) * gain).astype(jnp.bfloat16)
    logits = lax.dot_general(
        normed, router_ref[...], (((1,), (1,)), ((), ())), preferred_element_type=jnp.float32
    )
    peak = jnp.max(jnp.where(member, logits, -jnp.inf), axis=1, keepdims=True)
    mass = jnp.where(member, jnp.exp(logits - peak), 0.0)
    weights = mass / jnp.sum(mass, axis=1, keepdims=True)
    high = weights.astype(jnp.bfloat16).astype(jnp.float32)
    low = weights - high
    extra = jnp.concatenate(
        [high, low, jnp.zeros((2 * rows, LANES - 2 * experts), jnp.float32)], axis=1
    )
    for n in range(2):
        out_ref[n, :, :features] = normed[n * rows : (n + 1) * rows]
        out_ref[n, :, features:] = extra[n * rows : (n + 1) * rows].astype(jnp.bfloat16)


def expert_kernel(expert_count, near_ref, far_ref, gate, up, down, *refs):
    out_refs, hidden = refs[:-1], refs[-1]
    rows, features = out_refs[0].shape[1:]
    units = hidden.shape[1]
    near, other = [[ref[d].astype(jnp.float32) for d in range(ref.shape[0])] for ref in (near_ref, far_ref)]
    blocks = near + other
    order, kept = scatter_order(len(blocks)), gather_order(len(blocks))
    whole = jnp.concatenate([blocks[kept.index(k)] for k in order], axis=0)
    inputs = whole[:, :features].astype(jnp.bfloat16)
    packed = whole[:, features:]
    expert = lax.div(lax.axis_index("dev"), len(blocks) // expert_count)
    lane = lax.broadcasted_iota(jnp.int32, packed.shape, 1)
    mine = (lane % expert_count == expert) & (lane < 2 * expert_count)
    weight = jnp.sum(jnp.where(mine, packed, 0.0), axis=1, keepdims=True)

    def product(weights, cut):
        return jnp.dot(inputs, weights[:, cut], preferred_element_type=jnp.float32)

    for start in range(0, units, CHUNK):
        cut = slice(start, start + CHUNK)
        hidden[:, cut] = (jax.nn.silu(product(gate, cut)) * product(up, cut)).astype(jnp.bfloat16)
    for start in range(0, features, CHUNK):
        cut = slice(start, start + CHUNK)
        part = jnp.dot(hidden[...], down[:, cut], preferred_element_type=jnp.float32)
        send_blocks(out_refs, part * weight, cut, rows)


def stages_of(devices):
    stages, bit = [], 2
    while bit < devices:
        if bit > 2 and 2 * bit < devices:
            stages.append((bit, 2 * bit, 3 * bit))
            bit *= 4
        else:
            stages.append((bit,))
            bit *= 2
    return stages


def gather_order(devices):
    order = [0]
    for masks in stages_of(devices):
        order = order + [mask ^ k for mask in masks for k in order]
    return order + [1 ^ k for k in order]


def scatter_stages(devices):
    stages = stages_of(devices)
    return [(1,)] + stages[1:] + stages[:1]


def scatter_order(devices):
    return nested(scatter_stages(devices))


def nested(stages):
    order = [0]
    for masks in reversed(stages):
        order = order + [mask ^ k for mask in masks for k in order]
    return order


def hop(blocks, mask):
    devices = lax.axis_size("dev")
    return lax.ppermute(blocks, "dev", [(i, i ^ mask) for i in range(devices)])


def gather(block, idle):
    for masks in stages_of(lax.axis_size("dev"))[1:]:
        block = join([block] + [hop(block, mask) for mask in masks], idle)
    return block, hop(block, 1)


def join_kernel(count, *refs):
    size = refs[0].shape[0]
    for k in range(count):
        refs[-1][k * size : (k + 1) * size] = refs[k][...]


def join(parts, idle):
    shape = (len(parts) * parts[0].shape[0],) + parts[0].shape[1:]
    return pl.pallas_call(
        lambda *refs: join_kernel(len(parts), *refs),
        in_specs=[VMEM] * len(parts) + [HBM] * len(idle),
        out_specs=VMEM,
        out_shape=jax.ShapeDtypeStruct(shape, parts[0].dtype),
        compiler_params=params(8),
        name="join",
    )(*parts, *[far(a) for a in idle])


def scatter(keep, sends, idle, stages):
    for step, masks in enumerate(stages):
        parts = [keep] + [hop(block, mask) for block, mask in zip(sends, masks)]
        if step + 1 < len(stages):
            keep, *sends = fold(parts, len(stages[step + 1]) + 1, idle)
    return parts


def final_kernel(*refs):
    resid_ref, out_ref = refs[0], refs[-1]
    batches, sessions, _ = out_ref.shape
    mixed = resid_ref[...] + total_of(refs[1:-1])[0]
    for m in range(batches):
        out_ref[m] = mixed[m * sessions : (m + 1) * sessions].astype(jnp.bfloat16)


def exchange(blocks):
    devices = lax.axis_size("dev")
    groups = [list(range(core, devices, 2)) for core in range(2)]
    return lax.all_to_all(
        blocks, "dev", split_axis=0, concat_axis=0, axis_index_groups=groups, tiled=True
    )


def local(
    x_in,
    queries,
    cache_keys,
    cache_values,
    new_keys,
    new_values,
    lengths,
    w_out,
    norm_gain,
    w_router,
    experts_idx,
    w_gate,
    w_up,
    w_down,
):
    devices = lax.axis_size("dev")
    expert_count = w_router.shape[1]
    batches, sessions, features = x_in.shape
    rows = batches * sessions
    units = w_gate.shape[1]

    operands = [queries, cache_keys, new_keys, lengths, cache_values, new_values, w_out]
    heads, out_here = pl.pallas_call(
        attend_kernel,
        in_specs=[HBM] * len(operands),
        out_specs=(VMEM, VMEM),
        out_shape=(
            jax.ShapeDtypeStruct((devices // 2, rows, 2 * w_out.shape[0]), jnp.bfloat16),
            pltpu.VMEM(w_out.shape, w_out.dtype),
        ),
        scratch_shapes=[pltpu.VMEM(a.shape, a.dtype) for a in operands[:-1]]
        + [pltpu.SemaphoreType.DMA((len(operands),))],
        compiler_params=params(8),
        name="attend",
    )(*[far(a) for a in operands])
    head_blocks = exchange(heads)
    out_other = hop(w_out, 1)
    halves = [jax.ShapeDtypeStruct((devices // 2, rows, features), t) for t in (jnp.float32, jnp.bfloat16)]
    stages = scatter_stages(devices)
    first = (devices // 2) // (len(stages[1]) + 1)
    keep, *sends = pl.pallas_call(
        lambda *refs: project_kernel(nested(stages[1:]), *refs),
        in_specs=[VMEM] * 3 + [HBM],
        out_specs=[VMEM] * (len(stages[1]) + 1),
        out_shape=[jax.ShapeDtypeStruct((first, rows, features), jnp.float32)]
        + [jax.ShapeDtypeStruct((first, rows, features), jnp.bfloat16)] * len(stages[1]),
        compiler_params=params(8),
        name="project",
    )(head_blocks, here(out_here), here(out_other), far(w_gate))
    attn_parts = scatter(keep, sends, [w_gate], stages[1:-1])
    wide = jax.ShapeDtypeStruct((2, rows, features + LANES), jnp.bfloat16)
    keep, send = pl.pallas_call(
        lambda *refs: share_kernel(len(attn_parts), *refs),
        in_specs=[SMEM] + [VMEM] * (1 + len(attn_parts)) + [HBM],
        out_specs=(VMEM, VMEM),
        out_shape=(jax.ShapeDtypeStruct((2, rows, features), jnp.float32), wide),
        compiler_params=params(8),
        name="share",
    )(experts_idx, here(x_in), *attn_parts, far(w_gate))
    resid, message = pl.pallas_call(
        norm_kernel,
        in_specs=[VMEM] * 5 + [HBM],
        out_specs=(VMEM, VMEM),
        out_shape=(pltpu.VMEM((rows, features), jnp.float32), wide),
        compiler_params=params(8),
        name="norm",
    )(norm_gain, jnp.transpose(w_router), keep, send, hop(send, stages[-1][0]), far(w_gate))
    near, other = gather(message, [w_gate])
    keep, send = pl.pallas_call(
        lambda *refs: expert_kernel(expert_count, *refs),
        in_specs=[VMEM] * 5,
        out_specs=[VMEM] * 2,
        out_shape=halves,
        scratch_shapes=[
            pltpu.VMEM((devices * rows, units), jnp.bfloat16),
        ],
        compiler_params=params(8),
        name="experts",
    )(near, other, here(w_gate), here(w_up), here(w_down))
    parts = scatter(keep, [send], [], stages)
    return pl.pallas_call(
        final_kernel,
        in_specs=[VMEM] * (1 + len(parts)),
        out_specs=VMEM,
        out_shape=jax.ShapeDtypeStruct(x_in.shape, jnp.bfloat16),
        compiler_params=params(8),
        name="final",
    )(resid, *parts)


def solution(mesh):
    return jax.shard_map(
        local,
        mesh=mesh,
        in_specs=(
            P(None, ("groups", "dev"), None),
            P(None, ("groups", "dev"), None),
            P(None, ("groups", "dev"), None, None),
            P(None, ("groups", "dev"), None, None),
            P(None, ("groups", "dev"), None),
            P(None, ("groups", "dev"), None),
            P(None, ("groups", "dev")),
            P("dev", None),
            P(),
            P(),
            P(None, ("groups", "dev"), None),
            P(None, "dev"),
            P(None, "dev"),
            P("dev", None),
        ),
        out_specs=P(None, ("groups", "dev"), None),
        check_vma=False,
    )
```

```python
import math

import jax
import jax.numpy as jnp
from jax import lax
from jax.experimental import pallas as pl
from jax.experimental.pallas import tpu as pltpu
from jax.sharding import PartitionSpec as P

QH = 24
KVH = 4
HD = 128
LANES = 128
CHUNK = 512
MIB = 1 << 20

VMEM = pl.BlockSpec(memory_space=pltpu.VMEM)
HBM = pl.BlockSpec(memory_space=pltpu.HBM)


def params(mib):
    return pltpu.CompilerParams(vmem_limit_bytes=mib * MIB)


def attend_kernel(*refs):
    count = (len(refs) - 2) // 2
    operands, out_ref, w_ref = refs[:count], refs[count], refs[count + 1]
    buffers, sems = refs[count + 2 : -1] + (w_ref,), refs[-1]
    copies = [
        pltpu.make_async_copy(source, target, sems.at[i])
        for i, (source, target) in enumerate(zip(operands, buffers))
    ]
    for copy in copies:
        copy.start()
    q_ref, k_ref, nk_ref, len_ref, v_ref, nv_ref, _ = buffers
    for copy in copies[:4]:
        copy.wait()
    batches, sessions = q_ref.shape[:2]
    places = [(m, s) for m in range(batches) for s in range(sessions)]
    cache_len = k_ref.shape[2]
    width = KVH * HD
    per_kv = QH // KVH
    scale = 1.0 / math.sqrt(HD)
    head = lax.broadcasted_iota(jnp.int32, (QH, width), 0) // per_kv
    lane = lax.broadcasted_iota(jnp.int32, (QH, width), 1) // HD
    own_kv = jnp.concatenate([head == lane] * len(places), axis=0)
    slot = lax.broadcasted_iota(jnp.int32, (QH, cache_len), 1)

    def each(piece):
        return jnp.concatenate([piece(m, s) for m, s in places], axis=0)

    def spread(ref):
        full = [ref[m].astype(jnp.float32) for m in range(batches)]
        return each(lambda m, s: jnp.broadcast_to(full[m][s : s + 1], (QH, width)))

    q_all = [q_ref[m].astype(jnp.float32) for m in range(batches)]
    q_heads = jnp.concatenate(
        [q_all[m][s : s + 1, h * HD : (h + 1) * HD] for m, s in places for h in range(QH)], axis=0
    )
    q_wide = jnp.where(own_kv, jnp.concatenate([q_heads] * KVH, axis=1), 0.0)
    q_narrow = q_wide.astype(jnp.bfloat16)
    scores = scale * jnp.concatenate(
        [
            lax.dot_general(
                q_narrow[n * QH : (n + 1) * QH],
                k_ref[m, s],
                (((1,), (1,)), ((), ())),
                preferred_element_type=jnp.float32,
            )
            for n, (m, s) in enumerate(places)
        ],
        axis=0,
    )
    own_score = jnp.sum(q_wide * spread(nk_ref), axis=1, keepdims=True) * scale
    live = each(lambda m, s: slot - len_ref[m, s : s + 1][:, None]) < 0
    peak = jnp.maximum(
        jnp.max(jnp.where(live, scores, -jnp.inf), axis=1, keepdims=True), own_score
    )
    mass = jnp.where(live, jnp.exp(scores - peak), 0.0)
    own_mass = jnp.exp(own_score - peak)
    total = jnp.sum(mass, axis=1, keepdims=True) + own_mass
    probs = (mass / total).astype(jnp.bfloat16)
    own_prob = (own_mass / total).astype(jnp.bfloat16).astype(jnp.float32)
    for copy in copies[4:6]:
        copy.wait()
    wide = jnp.concatenate(
        [
            jnp.dot(
                probs[n * QH : (n + 1) * QH], v_ref[m, s], preferred_element_type=jnp.float32
            )
            for n, (m, s) in enumerate(places)
        ],
        axis=0,
    )
    wide = jnp.where(own_kv, wide + own_prob * spread(nv_ref), 0.0)
    heads = wide[:, :HD]
    for k in range(1, KVH):
        heads = heads + wide[:, k * HD : (k + 1) * HD]
    rows = [
        jnp.concatenate([heads[n * QH + h : n * QH + h + 1] for h in range(QH)], axis=1)
        for n in range(len(places))
    ]
    attention = jnp.concatenate(rows, axis=0).astype(jnp.bfloat16)
    devices, _, part = out_ref.shape
    for d in range(devices):
        out_ref[d] = attention[:, d * part : (d + 1) * part]
    copies[6].wait()


def far(array):
    return pltpu.with_memory_space_constraint(array, pltpu.HBM)


def here(array):
    return pltpu.with_memory_space_constraint(array, pltpu.VMEM)


def rows_of(ref, order):
    blocks = [ref[d].astype(jnp.float32) for d in order]
    return jnp.concatenate(blocks, axis=0)


def send_blocks(refs, value, cut, rows):
    at = 0
    for ref in refs:
        for k in range(ref.shape[0]):
            ref[k, :, cut] = value[at : at + rows].astype(ref.dtype)
            at += rows


def project_kernel(order, x_ref, w_ref, other_ref, _, *out_refs):
    rows, features = out_refs[0].shape[1:]
    half = w_ref.shape[0]
    me = lax.axis_index("dev")
    inputs = rows_of(x_ref, [lax.div(me ^ k, 2) for k in order])
    even = lax.rem(me, 2) == 0
    mine = jnp.where(even, inputs[:, :half], inputs[:, half:]).astype(jnp.bfloat16)
    others = jnp.where(even, inputs[:, half:], inputs[:, :half]).astype(jnp.bfloat16)
    for start in range(0, features, CHUNK):
        cut = slice(start, start + CHUNK)
        part = jnp.dot(mine, w_ref[:, cut], preferred_element_type=jnp.float32)
        part = part + jnp.dot(others, other_ref[:, cut], preferred_element_type=jnp.float32)
        send_blocks(out_refs, part, cut, rows)


def total_of(refs):
    total = refs[0][...].astype(jnp.float32)
    for ref in refs[1:]:
        total = total + ref[...].astype(jnp.float32)
    return total


def fold_kernel(count, outs, *refs):
    total = total_of(refs[:count])
    at = 0
    for ref in refs[-outs:]:
        ref[...] = total[at : at + ref.shape[0]].astype(ref.dtype)
        at += ref.shape[0]


def fold(parts, outs, idle):
    blocks, rows, features = parts[0].shape
    shape = (blocks // outs, rows, features)
    return pl.pallas_call(
        lambda *refs: fold_kernel(len(parts), outs, *refs),
        in_specs=[VMEM] * len(parts) + [HBM] * len(idle),
        out_specs=[VMEM] * outs,
        out_shape=[jax.ShapeDtypeStruct(shape, jnp.float32)]
        + [jax.ShapeDtypeStruct(shape, jnp.bfloat16)] * (outs - 1),
        compiler_params=params(8),
        name="fold",
    )(*parts, *[far(a) for a in idle])


def share_kernel(count, idx_ref, x_ref, *refs):
    keep_ref, out_ref = refs[-2:]
    batches, sessions, features = x_ref.shape
    rows = batches * sessions
    total = total_of(refs[:count])
    x_rows = jnp.concatenate([x_ref[m].astype(jnp.float32) for m in range(batches)], axis=0)
    own = total[0] + x_rows
    column = lax.broadcasted_iota(jnp.int32, (rows, LANES), 1)
    routes = jnp.concatenate([idx_ref[m] for m in range(batches)], axis=0)
    member = jnp.zeros((rows, LANES), jnp.float32)
    for k in range(routes.shape[1]):
        member = jnp.where(column == routes[:, k : k + 1], 1.0, member)
    keep_ref[0] = own
    keep_ref[1] = total[1]
    out_ref[0, :, :features] = own.astype(jnp.bfloat16)
    out_ref[1, :, :features] = total[1].astype(jnp.bfloat16)
    out_ref[0, :, features:] = member.astype(jnp.bfloat16)
    out_ref[1, :, features:] = jnp.zeros((rows, LANES), jnp.bfloat16)


def norm_kernel(gain_ref, router_ref, keep_ref, sent_ref, got_ref, *refs):
    resid_ref, out_ref = refs[-2:]
    rows, features = resid_ref.shape
    experts = router_ref.shape[0]
    got = got_ref[...].astype(jnp.float32)
    own = keep_ref[0] + got[1, :, :features]
    resid_ref[...] = own
    resid = jnp.concatenate([own, keep_ref[1] + got[0, :, :features]], axis=0)
    marks = jnp.concatenate([sent_ref[0, :, features:].astype(jnp.float32), got[0, :, features:]], axis=0)
    member = marks[:, :experts] > 0.5
    mean_square = jnp.mean(resid * resid, axis=1, keepdims=True)
    gain = gain_ref[...].astype(jnp.float32).reshape(1, features)
    normed = (resid * lax.rsqrt(mean_square + 1e-05) * gain).astype(jnp.bfloat16)
    logits = lax.dot_general(
        normed, router_ref[...], (((1,), (1,)), ((), ())), preferred_element_type=jnp.float32
    )
    peak = jnp.max(jnp.where(member, logits, -jnp.inf), axis=1, keepdims=True)
    mass = jnp.where(member, jnp.exp(logits - peak), 0.0)
    weights = mass / jnp.sum(mass, axis=1, keepdims=True)
    high = weights.astype(jnp.bfloat16).astype(jnp.float32)
    low = weights - high
    extra = jnp.concatenate(
        [high, low, jnp.zeros((2 * rows, LANES - 2 * experts), jnp.float32)], axis=1
    )
    for n in range(2):
        out_ref[n, :, :features] = normed[n * rows : (n + 1) * rows]
        out_ref[n, :, features:] = extra[n * rows : (n + 1) * rows].astype(jnp.bfloat16)


def expert_kernel(expert_count, near_ref, far_ref, gate, up, down, *refs):
    out_refs, hidden = refs[:-1], refs[-1]
    rows, features = out_refs[0].shape[1:]
    units = hidden.shape[1]
    near, other = [[ref[d].astype(jnp.float32) for d in range(ref.shape[0])] for ref in (near_ref, far_ref)]
    blocks = near + other
    order, kept = scatter_order(len(blocks)), gather_order(len(blocks))
    whole = jnp.concatenate([blocks[kept.index(k)] for k in order], axis=0)
    inputs = whole[:, :features].astype(jnp.bfloat16)
    packed = whole[:, features:]
    expert = lax.div(lax.axis_index("dev"), len(blocks) // expert_count)
    lane = lax.broadcasted_iota(jnp.int32, packed.shape, 1)
    mine = (lane % expert_count == expert) & (lane < 2 * expert_count)
    weight = jnp.sum(jnp.where(mine, packed, 0.0), axis=1, keepdims=True)

    def product(weights, cut):
        return jnp.dot(inputs, weights[:, cut], preferred_element_type=jnp.float32)

    for start in range(0, units, CHUNK):
        cut = slice(start, start + CHUNK)
        hidden[:, cut] = (jax.nn.silu(product(gate, cut)) * product(up, cut)).astype(jnp.bfloat16)
    for start in range(0, features, CHUNK):
        cut = slice(start, start + CHUNK)
        part = jnp.dot(hidden[...], down[:, cut], preferred_element_type=jnp.float32)
        send_blocks(out_refs, part * weight, cut, rows)


def stages_of(devices):
    stages, bit = [], 2
    while bit < devices:
        if bit > 2 and 2 * bit < devices:
            stages.append((bit, 2 * bit, 3 * bit))
            bit *= 4
        else:
            stages.append((bit,))
            bit *= 2
    return stages


def gather_order(devices):
    order = [0]
    for masks in stages_of(devices):
        order = order + [mask ^ k for mask in masks for k in order]
    return order + [1 ^ k for k in order]


def scatter_stages(devices):
    stages = stages_of(devices)
    return [(1,)] + stages[1:] + stages[:1]


def scatter_order(devices):
    return nested(scatter_stages(devices))


def nested(stages):
    order = [0]
    for masks in reversed(stages):
        order = order + [mask ^ k for mask in masks for k in order]
    return order


def hop(blocks, mask):
    devices = lax.axis_size("dev")
    return lax.ppermute(blocks, "dev", [(i, i ^ mask) for i in range(devices)])


def gather(block, idle):
    for masks in stages_of(lax.axis_size("dev"))[1:]:
        block = join([block] + [hop(block, mask) for mask in masks], idle)
    return block, hop(block, 1)


def join_kernel(count, *refs):
    size = refs[0].shape[0]
    for k in range(count):
        refs[-1][k * size : (k + 1) * size] = refs[k][...]


def join(parts, idle):
    shape = (len(parts) * parts[0].shape[0],) + parts[0].shape[1:]
    return pl.pallas_call(
        lambda *refs: join_kernel(len(parts), *refs),
        in_specs=[VMEM] * len(parts) + [HBM] * len(idle),
        out_specs=VMEM,
        out_shape=jax.ShapeDtypeStruct(shape, parts[0].dtype),
        compiler_params=params(8),
        name="join",
    )(*parts, *[far(a) for a in idle])


def scatter(keep, sends, idle, stages):
    for step, masks in enumerate(stages):
        parts = [keep] + [hop(block, mask) for block, mask in zip(sends, masks)]
        if step + 1 < len(stages):
            keep, *sends = fold(parts, len(stages[step + 1]) + 1, idle)
    return parts


def final_kernel(*refs):
    resid_ref, out_ref = refs[0], refs[-1]
    batches, sessions, _ = out_ref.shape
    mixed = resid_ref[...] + total_of(refs[1:-1])[0]
    for m in range(batches):
        out_ref[m] = mixed[m * sessions : (m + 1) * sessions].astype(jnp.bfloat16)


def exchange(blocks):
    devices = lax.axis_size("dev")
    groups = [list(range(core, devices, 2)) for core in range(2)]
    return lax.all_to_all(
        blocks, "dev", split_axis=0, concat_axis=0, axis_index_groups=groups, tiled=True
    )


def local(
    x_in,
    queries,
    cache_keys,
    cache_values,
    new_keys,
    new_values,
    lengths,
    w_out,
    norm_gain,
    w_router,
    experts_idx,
    w_gate,
    w_up,
    w_down,
):
    devices = lax.axis_size("dev")
    expert_count = w_router.shape[1]
    batches, sessions, features = x_in.shape
    rows = batches * sessions
    units = w_gate.shape[1]

    operands = [queries, cache_keys, new_keys, lengths, cache_values, new_values, w_out]
    heads, out_here = pl.pallas_call(
        attend_kernel,
        in_specs=[HBM] * len(operands),
        out_specs=(VMEM, VMEM),
        out_shape=(
            jax.ShapeDtypeStruct((devices // 2, rows, 2 * w_out.shape[0]), jnp.bfloat16),
            pltpu.VMEM(w_out.shape, w_out.dtype),
        ),
        scratch_shapes=[pltpu.VMEM(a.shape, a.dtype) for a in operands[:-1]]
        + [pltpu.SemaphoreType.DMA((len(operands),))],
        compiler_params=params(8),
        name="attend",
    )(*[far(a) for a in operands])
    head_blocks = exchange(heads)
    out_other = hop(w_out, 1)
    halves = [jax.ShapeDtypeStruct((devices // 2, rows, features), t) for t in (jnp.float32, jnp.bfloat16)]
    stages = scatter_stages(devices)
    first = (devices // 2) // (len(stages[1]) + 1)
    keep, *sends = pl.pallas_call(
        lambda *refs: project_kernel(nested(stages[1:]), *refs),
        in_specs=[VMEM] * 3 + [HBM],
        out_specs=[VMEM] * (len(stages[1]) + 1),
        out_shape=[jax.ShapeDtypeStruct((first, rows, features), jnp.float32)]
        + [jax.ShapeDtypeStruct((first, rows, features), jnp.bfloat16)] * len(stages[1]),
        compiler_params=params(8),
        name="project",
    )(head_blocks, here(out_here), here(out_other), far(w_gate))
    attn_parts = scatter(keep, sends, [w_gate], stages[1:-1])
    wide = jax.ShapeDtypeStruct((2, rows, features + LANES), jnp.bfloat16)
    keep, send = pl.pallas_call(
        lambda *refs: share_kernel(len(attn_parts), *refs),
        in_specs=[VMEM] * (2 + len(attn_parts)) + [HBM],
        out_specs=(VMEM, VMEM),
        out_shape=(jax.ShapeDtypeStruct((2, rows, features), jnp.float32), wide),
        compiler_params=params(8),
        name="share",
    )(here(experts_idx), here(x_in), *attn_parts, far(w_gate))
    resid, message = pl.pallas_call(
        norm_kernel,
        in_specs=[VMEM] * 5 + [HBM],
        out_specs=(VMEM, VMEM),
        out_shape=(pltpu.VMEM((rows, features), jnp.float32), wide),
        compiler_params=params(8),
        name="norm",
    )(norm_gain, jnp.transpose(w_router), keep, send, hop(send, stages[-1][0]), far(w_gate))
    near, other = gather(message, [w_gate])
    keep, send = pl.pallas_call(
        lambda *refs: expert_kernel(expert_count, *refs),
        in_specs=[VMEM] * 5,
        out_specs=[VMEM] * 2,
        out_shape=halves,
        scratch_shapes=[
            pltpu.VMEM((devices * rows, units), jnp.bfloat16),
        ],
        compiler_params=params(8),
        name="experts",
    )(near, other, here(w_gate), here(w_up), here(w_down))
    parts = scatter(keep, [send], [], stages)
    return pl.pallas_call(
        final_kernel,
        in_specs=[VMEM] * (1 + len(parts)),
        out_specs=VMEM,
        out_shape=jax.ShapeDtypeStruct(x_in.shape, jnp.bfloat16),
        compiler_params=params(8),
        name="final",
    )(resid, *parts)


def solution(mesh):
    return jax.shard_map(
        local,
        mesh=mesh,
        in_specs=(
            P(None, ("groups", "dev"), None),
            P(None, ("groups", "dev"), None),
            P(None, ("groups", "dev"), None, None),
            P(None, ("groups", "dev"), None, None),
            P(None, ("groups", "dev"), None),
            P(None, ("groups", "dev"), None),
            P(None, ("groups", "dev")),
            P("dev", None),
            P(),
            P(),
            P(None, ("groups", "dev"), None),
            P(None, "dev"),
            P(None, "dev"),
            P("dev", None),
        ),
        out_specs=P(None, ("groups", "dev"), None),
        check_vma=False,
    )
```

```python
import math

import jax
import jax.numpy as jnp
from jax import lax
from jax.experimental import pallas as pl
from jax.experimental.pallas import tpu as pltpu
from jax.sharding import PartitionSpec as P

QH = 24
KVH = 4
HD = 128
LANES = 128
CHUNK = 512
MIB = 1 << 20

VMEM = pl.BlockSpec(memory_space=pltpu.VMEM)
HBM = pl.BlockSpec(memory_space=pltpu.HBM)


def params(mib):
    return pltpu.CompilerParams(vmem_limit_bytes=mib * MIB)


def attend_kernel(*refs):
    count = (len(refs) - 2) // 2
    operands, out_ref, w_ref = refs[:count], refs[count], refs[count + 1]
    buffers, sems = refs[count + 2 : -1] + (w_ref,), refs[-1]
    copies = [
        pltpu.make_async_copy(source, target, sems.at[i])
        for i, (source, target) in enumerate(zip(operands, buffers))
    ]
    for copy in copies:
        copy.start()
    q_ref, k_ref, nk_ref, len_ref, v_ref, nv_ref, _ = buffers
    for copy in copies[:4]:
        copy.wait()
    batches, sessions = q_ref.shape[:2]
    places = [(m, s) for m in range(batches) for s in range(sessions)]
    cache_len = k_ref.shape[2]
    width = KVH * HD
    per_kv = QH // KVH
    scale = 1.0 / math.sqrt(HD)
    head = lax.broadcasted_iota(jnp.int32, (QH, width), 0) // per_kv
    lane = lax.broadcasted_iota(jnp.int32, (QH, width), 1) // HD
    own_kv = jnp.concatenate([head == lane] * len(places), axis=0)
    slot = lax.broadcasted_iota(jnp.int32, (QH, cache_len), 1)

    def each(piece):
        return jnp.concatenate([piece(m, s) for m, s in places], axis=0)

    def spread(ref):
        full = [ref[m].astype(jnp.float32) for m in range(batches)]
        return each(lambda m, s: jnp.broadcast_to(full[m][s : s + 1], (QH, width)))

    q_all = [q_ref[m].astype(jnp.float32) for m in range(batches)]
    q_heads = jnp.concatenate(
        [q_all[m][s : s + 1, h * HD : (h + 1) * HD] for m, s in places for h in range(QH)], axis=0
    )
    q_wide = jnp.where(own_kv, jnp.concatenate([q_heads] * KVH, axis=1), 0.0)
    q_narrow = q_wide.astype(jnp.bfloat16)
    scores = scale * jnp.concatenate(
        [
            lax.dot_general(
                q_narrow[n * QH : (n + 1) * QH],
                k_ref[m, s],
                (((1,), (1,)), ((), ())),
                preferred_element_type=jnp.float32,
            )
            for n, (m, s) in enumerate(places)
        ],
        axis=0,
    )
    own_score = jnp.sum(q_wide * spread(nk_ref), axis=1, keepdims=True) * scale
    live = each(lambda m, s: slot - len_ref[m, s : s + 1][:, None]) < 0
    peak = jnp.maximum(
        jnp.max(jnp.where(live, scores, -jnp.inf), axis=1, keepdims=True), own_score
    )
    mass = jnp.where(live, jnp.exp(scores - peak), 0.0)
    own_mass = jnp.exp(own_score - peak)
    total = jnp.sum(mass, axis=1, keepdims=True) + own_mass
    probs = (mass / total).astype(jnp.bfloat16)
    own_prob = (own_mass / total).astype(jnp.bfloat16).astype(jnp.float32)
    for copy in copies[4:6]:
        copy.wait()
    wide = jnp.concatenate(
        [
            jnp.dot(
                probs[n * QH : (n + 1) * QH], v_ref[m, s], preferred_element_type=jnp.float32
            )
            for n, (m, s) in enumerate(places)
        ],
        axis=0,
    )
    wide = jnp.where(own_kv, wide + own_prob * spread(nv_ref), 0.0)
    heads = wide[:, :HD]
    for k in range(1, KVH):
        heads = heads + wide[:, k * HD : (k + 1) * HD]
    rows = [
        jnp.concatenate([heads[n * QH + h : n * QH + h + 1] for h in range(QH)], axis=1)
        for n in range(len(places))
    ]
    attention = jnp.concatenate(rows, axis=0).astype(jnp.bfloat16)
    devices, _, part = out_ref.shape
    for d in range(devices):
        out_ref[d] = attention[:, d * part : (d + 1) * part]
    copies[6].wait()


def far(array):
    return pltpu.with_memory_space_constraint(array, pltpu.HBM)


def here(array):
    return pltpu.with_memory_space_constraint(array, pltpu.VMEM)


def rows_of(ref, order):
    blocks = [ref[d].astype(jnp.float32) for d in order]
    return jnp.concatenate(blocks, axis=0)


def send_blocks(refs, value, cut, rows):
    at = 0
    for ref in refs:
        for k in range(ref.shape[0]):
            ref[k, :, cut] = value[at : at + rows].astype(ref.dtype)
            at += rows


def project_kernel(order, x_ref, w_ref, other_ref, _, *out_refs):
    rows, features = out_refs[0].shape[1:]
    half = w_ref.shape[0]
    me = lax.axis_index("dev")
    inputs = rows_of(x_ref, [lax.div(me ^ k, 2) for k in order])
    even = lax.rem(me, 2) == 0
    mine = jnp.where(even, inputs[:, :half], inputs[:, half:]).astype(jnp.bfloat16)
    others = jnp.where(even, inputs[:, half:], inputs[:, :half]).astype(jnp.bfloat16)
    for start in range(0, features, CHUNK):
        cut = slice(start, start + CHUNK)
        part = jnp.dot(mine, w_ref[:, cut], preferred_element_type=jnp.float32)
        part = part + jnp.dot(others, other_ref[:, cut], preferred_element_type=jnp.float32)
        send_blocks(out_refs, part, cut, rows)


def total_of(refs):
    total = refs[0][...].astype(jnp.float32)
    for ref in refs[1:]:
        total = total + ref[...].astype(jnp.float32)
    return total


def fold_kernel(count, outs, *refs):
    total = total_of(refs[:count])
    at = 0
    for ref in refs[-outs:]:
        ref[...] = total[at : at + ref.shape[0]].astype(ref.dtype)
        at += ref.shape[0]


def fold(parts, outs, idle):
    blocks, rows, features = parts[0].shape
    shape = (blocks // outs, rows, features)
    return pl.pallas_call(
        lambda *refs: fold_kernel(len(parts), outs, *refs),
        in_specs=[VMEM] * len(parts) + [HBM] * len(idle),
        out_specs=[VMEM] * outs,
        out_shape=[jax.ShapeDtypeStruct(shape, jnp.float32)]
        + [jax.ShapeDtypeStruct(shape, jnp.bfloat16)] * (outs - 1),
        compiler_params=params(8),
        name="fold",
    )(*parts, *[far(a) for a in idle])


def share_kernel(count, idx_ref, x_ref, *refs):
    keep_ref, out_ref = refs[-2:]
    batches, sessions, features = x_ref.shape
    rows = batches * sessions
    total = total_of(refs[:count])
    x_rows = jnp.concatenate([x_ref[m].astype(jnp.float32) for m in range(batches)], axis=0)
    own = total[0] + x_rows
    column = lax.broadcasted_iota(jnp.int32, (rows, LANES), 1)
    routes = jnp.concatenate([idx_ref[m] for m in range(batches)], axis=0)
    member = jnp.zeros((rows, LANES), jnp.float32)
    for k in range(routes.shape[1]):
        member = jnp.where(column == routes[:, k : k + 1], 1.0, member)
    keep_ref[0] = own
    keep_ref[1] = total[1]
    out_ref[0, :, :features] = own.astype(jnp.bfloat16)
    out_ref[1, :, :features] = total[1].astype(jnp.bfloat16)
    out_ref[0, :, features:] = member.astype(jnp.bfloat16)
    out_ref[1, :, features:] = jnp.zeros((rows, LANES), jnp.bfloat16)


def norm_kernel(gain_ref, router_ref, keep_ref, sent_ref, got_ref, *refs):
    resid_ref, out_ref = refs[-2:]
    rows, features = resid_ref.shape
    experts = router_ref.shape[0]
    got = got_ref[...].astype(jnp.float32)
    own = keep_ref[0] + got[1, :, :features]
    resid_ref[...] = own
    resid = jnp.concatenate([own, keep_ref[1] + got[0, :, :features]], axis=0)
    marks = jnp.concatenate([sent_ref[0, :, features:].astype(jnp.float32), got[0, :, features:]], axis=0)
    member = marks[:, :experts] > 0.5
    mean_square = jnp.mean(resid * resid, axis=1, keepdims=True)
    gain = gain_ref[...].astype(jnp.float32).reshape(1, features)
    normed = (resid * lax.rsqrt(mean_square + 1e-05) * gain).astype(jnp.bfloat16)
    logits = lax.dot_general(
        normed, router_ref[...], (((1,), (1,)), ((), ())), preferred_element_type=jnp.float32
    )
    peak = jnp.max(jnp.where(member, logits, -jnp.inf), axis=1, keepdims=True)
    mass = jnp.where(member, jnp.exp(logits - peak), 0.0)
    weights = mass / jnp.sum(mass, axis=1, keepdims=True)
    high = weights.astype(jnp.bfloat16).astype(jnp.float32)
    low = weights - high
    extra = jnp.concatenate(
        [high, low, jnp.zeros((2 * rows, LANES - 2 * experts), jnp.float32)], axis=1
    )
    for n in range(2):
        out_ref[n, :, :features] = normed[n * rows : (n + 1) * rows]
        out_ref[n, :, features:] = extra[n * rows : (n + 1) * rows].astype(jnp.bfloat16)


def expert_kernel(expert_count, near_ref, far_ref, gate, up, down, *refs):
    out_refs, hidden = refs[:-1], refs[-1]
    rows, features = out_refs[0].shape[1:]
    units = hidden.shape[1]
    near, other = [[ref[d].astype(jnp.float32) for d in range(ref.shape[0])] for ref in (near_ref, far_ref)]
    blocks = near + other
    order, kept = scatter_order(len(blocks)), gather_order(len(blocks))
    whole = jnp.concatenate([blocks[kept.index(k)] for k in order], axis=0)
    inputs = whole[:, :features].astype(jnp.bfloat16)
    packed = whole[:, features:]
    expert = lax.div(lax.axis_index("dev"), len(blocks) // expert_count)
    lane = lax.broadcasted_iota(jnp.int32, packed.shape, 1)
    mine = (lane % expert_count == expert) & (lane < 2 * expert_count)
    weight = jnp.sum(jnp.where(mine, packed, 0.0), axis=1, keepdims=True)

    def product(weights, cut):
        return jnp.dot(inputs, weights[:, cut], preferred_element_type=jnp.float32)

    for start in range(0, units, CHUNK):
        cut = slice(start, start + CHUNK)
        hidden[:, cut] = (jax.nn.silu(product(gate, cut)) * product(up, cut)).astype(jnp.bfloat16)
    for start in range(0, features, CHUNK):
        cut = slice(start, start + CHUNK)
        part = jnp.dot(hidden[...], down[:, cut], preferred_element_type=jnp.float32)
        send_blocks(out_refs, part * weight, cut, rows)


def stages_of(devices):
    stages, bit = [], 2
    while bit < devices:
        if bit > 2 and 2 * bit < devices:
            stages.append((3 * bit, 2 * bit, bit))
            bit *= 4
        else:
            stages.append((bit,))
            bit *= 2
    return stages


def gather_order(devices):
    order = [0]
    for masks in stages_of(devices):
        order = order + [mask ^ k for mask in masks for k in order]
    return order + [1 ^ k for k in order]


def scatter_stages(devices):
    stages = stages_of(devices)
    return [(1,)] + stages[1:] + stages[:1]


def scatter_order(devices):
    return nested(scatter_stages(devices))


def nested(stages):
    order = [0]
    for masks in reversed(stages):
        order = order + [mask ^ k for mask in masks for k in order]
    return order


def hop(blocks, mask):
    devices = lax.axis_size("dev")
    return lax.ppermute(blocks, "dev", [(i, i ^ mask) for i in range(devices)])


def gather(block, idle):
    for masks in stages_of(lax.axis_size("dev"))[1:]:
        block = join([block] + [hop(block, mask) for mask in masks], idle)
    return block, hop(block, 1)


def join_kernel(count, *refs):
    size = refs[0].shape[0]
    for k in range(count):
        refs[-1][k * size : (k + 1) * size] = refs[k][...]


def join(parts, idle):
    shape = (len(parts) * parts[0].shape[0],) + parts[0].shape[1:]
    return pl.pallas_call(
        lambda *refs: join_kernel(len(parts), *refs),
        in_specs=[VMEM] * len(parts) + [HBM] * len(idle),
        out_specs=VMEM,
        out_shape=jax.ShapeDtypeStruct(shape, parts[0].dtype),
        compiler_params=params(8),
        name="join",
    )(*parts, *[far(a) for a in idle])


def scatter(keep, sends, idle, stages):
    for step, masks in enumerate(stages):
        parts = [keep] + [hop(block, mask) for block, mask in zip(sends, masks)]
        if step + 1 < len(stages):
            keep, *sends = fold(parts, len(stages[step + 1]) + 1, idle)
    return parts


def final_kernel(*refs):
    resid_ref, out_ref = refs[0], refs[-1]
    batches, sessions, _ = out_ref.shape
    mixed = resid_ref[...] + total_of(refs[1:-1])[0]
    for m in range(batches):
        out_ref[m] = mixed[m * sessions : (m + 1) * sessions].astype(jnp.bfloat16)


def exchange(blocks):
    devices = lax.axis_size("dev")
    groups = [list(range(core, devices, 2)) for core in range(2)]
    return lax.all_to_all(
        blocks, "dev", split_axis=0, concat_axis=0, axis_index_groups=groups, tiled=True
    )


def local(
    x_in,
    queries,
    cache_keys,
    cache_values,
    new_keys,
    new_values,
    lengths,
    w_out,
    norm_gain,
    w_router,
    experts_idx,
    w_gate,
    w_up,
    w_down,
):
    devices = lax.axis_size("dev")
    expert_count = w_router.shape[1]
    batches, sessions, features = x_in.shape
    rows = batches * sessions
    units = w_gate.shape[1]

    operands = [queries, cache_keys, new_keys, lengths, cache_values, new_values, w_out]
    heads, out_here = pl.pallas_call(
        attend_kernel,
        in_specs=[HBM] * len(operands),
        out_specs=(VMEM, VMEM),
        out_shape=(
            jax.ShapeDtypeStruct((devices // 2, rows, 2 * w_out.shape[0]), jnp.bfloat16),
            pltpu.VMEM(w_out.shape, w_out.dtype),
        ),
        scratch_shapes=[pltpu.VMEM(a.shape, a.dtype) for a in operands[:-1]]
        + [pltpu.SemaphoreType.DMA((len(operands),))],
        compiler_params=params(8),
        name="attend",
    )(*[far(a) for a in operands])
    head_blocks = exchange(heads)
    out_other = hop(w_out, 1)
    halves = [jax.ShapeDtypeStruct((devices // 2, rows, features), t) for t in (jnp.float32, jnp.bfloat16)]
    stages = scatter_stages(devices)
    first = (devices // 2) // (len(stages[1]) + 1)
    keep, *sends = pl.pallas_call(
        lambda *refs: project_kernel(nested(stages[1:]), *refs),
        in_specs=[VMEM] * 3 + [HBM],
        out_specs=[VMEM] * (len(stages[1]) + 1),
        out_shape=[jax.ShapeDtypeStruct((first, rows, features), jnp.float32)]
        + [jax.ShapeDtypeStruct((first, rows, features), jnp.bfloat16)] * len(stages[1]),
        compiler_params=params(8),
        name="project",
    )(head_blocks, here(out_here), here(out_other), far(w_gate))
    attn_parts = scatter(keep, sends, [w_gate], stages[1:-1])
    wide = jax.ShapeDtypeStruct((2, rows, features + LANES), jnp.bfloat16)
    keep, send = pl.pallas_call(
        lambda *refs: share_kernel(len(attn_parts), *refs),
        in_specs=[VMEM] * (2 + len(attn_parts)) + [HBM],
        out_specs=(VMEM, VMEM),
        out_shape=(jax.ShapeDtypeStruct((2, rows, features), jnp.float32), wide),
        compiler_params=params(8),
        name="share",
    )(here(experts_idx), here(x_in), *attn_parts, far(w_gate))
    resid, message = pl.pallas_call(
        norm_kernel,
        in_specs=[VMEM] * 5 + [HBM],
        out_specs=(VMEM, VMEM),
        out_shape=(pltpu.VMEM((rows, features), jnp.float32), wide),
        compiler_params=params(8),
        name="norm",
    )(norm_gain, jnp.transpose(w_router), keep, send, hop(send, stages[-1][0]), far(w_gate))
    near, other = gather(message, [w_gate])
    keep, send = pl.pallas_call(
        lambda *refs: expert_kernel(expert_count, *refs),
        in_specs=[VMEM] * 5,
        out_specs=[VMEM] * 2,
        out_shape=halves,
        scratch_shapes=[
            pltpu.VMEM((devices * rows, units), jnp.bfloat16),
        ],
        compiler_params=params(8),
        name="experts",
    )(near, other, here(w_gate), here(w_up), here(w_down))
    parts = scatter(keep, [send], [], stages)
    return pl.pallas_call(
        final_kernel,
        in_specs=[VMEM] * (1 + len(parts)),
        out_specs=VMEM,
        out_shape=jax.ShapeDtypeStruct(x_in.shape, jnp.bfloat16),
        compiler_params=params(8),
        name="final",
    )(resid, *parts)


def solution(mesh):
    return jax.shard_map(
        local,
        mesh=mesh,
        in_specs=(
            P(None, ("groups", "dev"), None),
            P(None, ("groups", "dev"), None),
            P(None, ("groups", "dev"), None, None),
            P(None, ("groups", "dev"), None, None),
            P(None, ("groups", "dev"), None),
            P(None, ("groups", "dev"), None),
            P(None, ("groups", "dev")),
            P("dev", None),
            P(),
            P(),
            P(None, ("groups", "dev"), None),
            P(None, "dev"),
            P(None, "dev"),
            P("dev", None),
        ),
        out_specs=P(None, ("groups", "dev"), None),
        check_vma=False,
    )
```
